32 devices in a mesh: dp: 32 (over z, y, x, core).
Axes of the slice: x: 2, y: 2, z: 4, core: 2. Of those that a mesh axis runs over, the one named last changes fastest.
Arguments:
- inputs: bfloat16 [128, 199, 512], P('dp'), may hold values from -6 to 6
- weights: bfloat16 [2, 262144], replicated, may hold values from -0.1875 to 0.1875
- ln_gain: float32 [512], replicated, may hold values from 0.45 to 2.16
- ln_bias: float32 [512], replicated, may hold values from -3 to 3
- projection: bfloat16 [512, 1024], replicated, may hold values from -0.25 to 0.25
- targets: float32 [128, 1024], P('dp'), may hold values from -6 to 6
- master: float32 [2, 262144], P(None, 'dp'), may hold values from -0.006 to 0.006
- first_moment: float32 [2, 262144], P(None, 'dp'), may hold values from -0.0006 to 0.0006
- second_moment: float32 [2, 262144], P(None, 'dp'), may hold values from 1e-11 to 1e-08
Outputs:
- input_grad: bfloat16 [128, 199, 512], P('dp')
- update: float32 [2, 262144], P(None, 'dp')
- new_master: float32 [2, 262144], P(None, 'dp')
- new_first: float32 [2, 262144], P(None, 'dp')
- new_second: float32 [2, 262144], P(None, 'dp')
- new_weights: bfloat16 [2, 262144], replicated
The draws below stay inside these ranges and needn't reach their ends.
All inputs are finite; a program needn't handle non-finite values.
Results may differ from the reference program's by a relative error of at most 0.006.
Values may be sent and summed in bfloat16 or wider, within the bound.
A program may use at most 64 MiB of HBM per device.

```python
import math
import jax
import jax.numpy as jnp
from jax import lax

C = 512
E = 1024
KW = 2
FIN = 199
CLIPS = 4
BATCH = 128
N_DP = 32


def draw_ln_gain(key, part):
    inner = jax.random.fold_in(key, 11)
    ramp = 0.6 + 1.2 * jnp.arange(C, dtype=jnp.float32) / (C - 1)
    jitter = jax.random.uniform(inner, (C,), jnp.float32, 0.8, 1.2)
    return ramp * jitter


def shard_levels(own_key, extent, shards, low, top_value):
    loudness, own = 1.0, jax.random.fold_in(own_key, 6)
    for dim, shards_of in shards:
        heights = jnp.exp(jax.random.uniform(jax.random.fold_in(own, dim), (shards_of,), jnp.float32, low / len(shards), top_value / len(shards)))
        loudness = loudness * jnp.repeat(heights, extent[dim] // shards_of).reshape([-1 if axis == dim else 1 for axis in range(len(extent))])
    return loudness


def bell_draw(key, shape, deviation, reach, split=(), held_as=jnp.bfloat16):
    level = shard_levels(key, shape, split, -0.22, 0.18) if split else 1.0
    entries = jax.random.normal(key, shape, jnp.float32) * deviation * level
    return jnp.minimum(jnp.maximum(entries, -reach), reach).astype(held_as)


def setup_inputs(seed: int = 0) -> dict:
    seeds = jax.random.split(jax.random.key(seed), 10)
    inputs = bell_draw(seeds[0], (BATCH, FIN, C), 1.0, 6.0, ((0, 32),))
    weights = bell_draw(seeds[1], (KW, C * C), (KW * C) ** -0.5, 0.1875)
    ln_gain = draw_ln_gain(jax.random.fold_in(seeds[9], 71), 0)
    ln_bias = bell_draw(seeds[3], (C,), 0.5, 3.0, (), jnp.float32)
    projection = bell_draw(seeds[4], (C, E), C ** -0.5, 0.25)
    targets = bell_draw(seeds[5], (BATCH, E), 1.0, 6.0, ((0, 32),), jnp.float32)
    master = bell_draw(seeds[6], (KW, C * C), 0.001, 0.006, ((1, 32),), jnp.float32)
    first_moment = bell_draw(seeds[7], (KW, C * C), 0.0001, 0.0006, ((1, 32),), jnp.float32)
    second_moment = jnp.clip(jnp.exp(math.log(9.99999993922529e-09) - 6.9077553 * jax.random.uniform(seeds[8], (KW, C * C), jnp.float32) ** shard_levels(seeds[8], (KW, C * C), ((1, 32),), -0.2, 0.2)), 9.999999960041972e-12, 9.99999993922529e-09)
    return {"inputs": inputs, "weights": weights, "ln_gain": ln_gain, "ln_bias": ln_bias, "projection": projection, "targets": targets, "master": master, "first_moment": first_moment, "second_moment": second_moment}


def norm_act(pre, gain, bias):
    center = pre - lax.optimization_barrier(jnp.mean(pre, axis=-1, keepdims=True))
    spread = lax.optimization_barrier(jnp.mean(center * center, axis=-1, keepdims=True))
    normed = center * lax.rsqrt(spread + 1e-05)
    return jax.nn.gelu(normed * gain + bias, approximate=False)

def local_pass(inputs, weights, ln_gain, ln_bias, projection, targets):
    clips, frames_in, chans = inputs.shape
    taps = weights.shape[0]
    frames_out = (frames_in - taps) // taps + 1
    windows = inputs[:, :frames_out * taps].reshape(clips, frames_out, taps, chans)
    kernel = weights.reshape(taps, chans, chans)
    pre = jnp.einsum('bfki,koi->bfo', windows.astype(jnp.float32), kernel.astype(jnp.float32))
    act, pull = jax.vjp(lambda value: norm_act(value, ln_gain, ln_bias), pre)
    pooled = lax.optimization_barrier(jnp.mean(act, axis=1)).astype(jnp.bfloat16)
    predicted = jnp.dot(pooled, projection, preferred_element_type=jnp.float32)
    miss = (predicted - targets).astype(jnp.bfloat16)
    back = jnp.dot(miss, projection.T, preferred_element_type=jnp.float32)
    upstream = jnp.broadcast_to(back[:, None, :] / frames_out, act.shape)
    dpre = pull(upstream)[0].astype(jnp.bfloat16)
    dwin = jnp.einsum('bfo,koi->bfki', dpre.astype(jnp.float32), kernel.astype(jnp.float32)).astype(jnp.bfloat16)
    dinput = dwin.reshape(clips, frames_out * taps, chans)
    tail = jnp.zeros((clips, frames_in - frames_out * taps, chans), jnp.bfloat16)
    return (windows, dpre, jnp.concatenate([dinput, tail], axis=1))

def reference(inputs, weights, ln_gain, ln_bias, projection, targets, master, first_moment, second_moment):
    groups = inputs.reshape(N_DP, CLIPS, FIN, C)
    goals = targets.reshape(N_DP, CLIPS, E)

    def one_group(total, pair):
        windows, dpre, dinput = local_pass(pair[0], weights, ln_gain, ln_bias, projection, pair[1])
        term = jnp.einsum('bfo,bfki->koi', dpre.astype(jnp.float32), windows.astype(jnp.float32))
        return (total + term, dinput)
    start = jnp.zeros((KW, C, C), jnp.float32)
    grad, dinputs = lax.scan(one_group, start, (groups, goals))
    grad = grad.reshape(KW, C * C)
    norm_total = jnp.sqrt(jnp.sum(grad * grad))
    scale = jnp.minimum(1.0, 1.0 / (norm_total + 1e-06))
    clipped = scale * grad
    new_first = 0.9 * first_moment + 0.1 * clipped
    new_second = 0.999 * second_moment + 0.001 * clipped * clipped
    update = new_first / (1.0 - 0.9 ** 20) / (jnp.sqrt(new_second / (1.0 - 0.999 ** 20)) + 1e-08)
    new_master = master - 0.0001 * (update + 0.01 * master)
    new_weights = new_master.astype(jnp.bfloat16)
    return (dinputs.reshape(BATCH, FIN, C), update, new_master, new_first, new_second, new_weights)
```

```python
import functools

import jax
import jax.numpy as jnp
from jax import lax
from jax.experimental import pallas as pl
from jax.experimental.pallas import tpu as pltpu
from jax.sharding import PartitionSpec as P

MESH = pl.DeviceIdType.MESH
LANES = 128
F32 = jnp.float32
BF16 = jnp.bfloat16


def norm_act(pre, gain, bias):
    center = pre - jnp.mean(pre, axis=-1, keepdims=True)
    spread = jnp.mean(center * center, axis=-1, keepdims=True)
    normed = center * lax.rsqrt(spread + 1e-05)
    return jax.nn.gelu(normed * gain + bias, approximate=False)


def local_pass(inputs, weights, ln_gain, ln_bias, projection, targets):
    clips, frames_in, chans = inputs.shape
    taps = weights.shape[0]
    frames_out = (frames_in - taps) // taps + 1
    windows = inputs[:, : frames_out * taps].reshape(clips, frames_out, taps, chans)
    kernel = weights.reshape(taps, chans, chans)
    pre = jnp.einsum("bfki,koi->bfo", windows, kernel, preferred_element_type=jnp.float32)
    act, pull = jax.vjp(lambda value: norm_act(value, ln_gain, ln_bias), pre)
    pooled = jnp.mean(act, axis=1).astype(jnp.bfloat16)
    predicted = jnp.dot(pooled, projection, preferred_element_type=jnp.float32)
    miss = (predicted - targets).astype(jnp.bfloat16)
    back = lax.dot_general(
        miss, projection, (((1,), (1,)), ((), ())), preferred_element_type=jnp.float32
    )
    upstream = jnp.broadcast_to(back[:, None, :] / frames_out, act.shape)
    dpre = pull(upstream)[0].astype(jnp.bfloat16)
    dwin = jnp.einsum("bfo,koi->bfki", dpre, kernel, preferred_element_type=jnp.float32).astype(
        jnp.bfloat16
    )
    dinput = dwin.reshape(clips, frames_out * taps, chans)
    tail = jnp.zeros((clips, frames_in - frames_out * taps, chans), jnp.bfloat16)
    return (windows, dpre, jnp.concatenate([dinput, tail], axis=1))


def adamw(grad, scale, master, first_moment, second_moment):
    clipped = scale * grad
    new_first = 0.9 * first_moment + 0.1 * clipped
    new_second = 0.999 * second_moment + 0.001 * clipped * clipped
    update = new_first / (1.0 - 0.9**20) / (jnp.sqrt(new_second / (1.0 - 0.999**20)) + 1e-08)
    new_master = master - 0.0001 * (update + 0.01 * master)
    return update, new_master, new_first, new_second


def plain_body(
    inputs, weights, ln_gain, ln_bias, projection, targets, master, first_moment, second_moment
):
    windows, dpre, input_grad = local_pass(inputs, weights, ln_gain, ln_bias, projection, targets)
    taps = weights.shape[0]
    term = jnp.einsum("bfo,bfki->koi", dpre, windows, preferred_element_type=jnp.float32)
    grad = lax.psum_scatter(term.reshape(taps, -1), "dp", scatter_dimension=1, tiled=True)
    squares = lax.psum(jnp.sum(grad * grad), "dp")
    scale = jnp.minimum(1.0, 1.0 / (jnp.sqrt(squares) + 1e-06))
    update, new_master, new_first, new_second = adamw(
        grad, scale, master, first_moment, second_moment
    )
    new_weights = lax.all_gather(new_master.astype(jnp.bfloat16), "dp", axis=1, tiled=True)
    return (input_grad, update, new_master, new_first, new_second, new_weights)


def dot(a, b, dims):
    return lax.dot_general(a, b, (dims, ((), ())), preferred_element_type=F32)


def step_kernel(
    n, frames_out,
    inputs, kern, gain_ref, bias_ref, projection, targets, master, first, second,
    dinput, update, new_master, new_first, new_second, gathered,
    frames32, win, slope, normed, dpre_ref, term,
    out0, in0, out1, in1, out2, in2, out3, in3, sq_out, sq_in, grad,
    s0, r0, s1, r1, s2, r2, s3, r3, sq_s, sq_r, zs_s, zs_r, xs, xr, ys, yr, dxs, dxr, dys, dyr,
    cs, cr,
):
    clips, frames_in, chans = inputs.shape
    tiles = chans // LANES
    fpad = win.shape[1] // clips
    rows = grad.shape[1] // chans
    width = grad.shape[1]
    depth = n // 8

    me = lax.axis_index("dp")
    c = me % 2
    x = (me // 2) % 2
    y = (me // 4) % 2
    z = me // 8
    core_peer = me + 1 - 2 * c
    x_peer = me + 2 - 4 * x
    y_peer = me + 4 - 8 * y

    barrier = pltpu.get_barrier_semaphore()
    for j in range(1, n):
        pl.semaphore_signal(barrier, inc=1, device_id=((me + j) % n,), device_id_type=MESH)

    for b in range(clips):
        for l in range(tiles):
            lanes = slice(l * LANES, (l + 1) * LANES)
            frames32[b, l, 0:frames_in, :] = inputs[b, :, lanes].astype(F32)
            frames32[b, l, 2 * frames_out : 2 * fpad, :] = jnp.zeros(
                (2 * fpad - 2 * frames_out, LANES), F32
            )
            for t in range(2):
                win[t, b * fpad : (b + 1) * fpad, lanes] = frames32[
                    b, l, pl.ds(t, fpad, stride=2), :
                ].astype(BF16)

    gain = gain_ref[...]
    bias = bias_ref[...]
    live = lax.broadcasted_iota(jnp.int32, (fpad, 1), 0) < frames_out
    means = []
    invs = []
    for b in range(clips):
        part = slice(b * fpad, (b + 1) * fpad)
        pre = dot(win[0, part, :], kern[0], ((1,), (1,))) + dot(
            win[1, part, :], kern[1], ((1,), (1,))
        )
        center = pre - jnp.mean(pre, axis=-1, keepdims=True)
        spread = jnp.mean(center * center, axis=-1, keepdims=True)
        inv = lax.rsqrt(spread + 1e-05)
        nrm = center * inv
        h = nrm * gain + bias
        cdf = 0.5 + 0.5 * lax.erf(h * (0.5**0.5))
        act = jnp.where(live, h * cdf, 0.0)
        pdf = jnp.exp(-0.5 * h * h) * 0.3989422804014327
        slope[part, :] = jnp.where(live, (cdf + h * pdf) * gain, 0.0)
        normed[part, :] = nrm
        means.append(jnp.sum(act, axis=0, keepdims=True) / frames_out)
        invs.append(inv)
    pooled = jnp.concatenate(means, axis=0).astype(BF16)
    predicted = dot(pooled, projection[...], ((1,), (0,)))
    miss = (predicted - targets[...]).astype(BF16)
    back = dot(miss, projection[...], ((1,), (1,))) / frames_out
    for b in range(clips):
        part = slice(b * fpad, (b + 1) * fpad)
        nrm = normed[part, :]
        dn = slope[part, :] * back[b : b + 1, :]
        low = jnp.mean(dn, axis=-1, keepdims=True)
        tilt = jnp.mean(dn * nrm, axis=-1, keepdims=True)
        dpre_ref[part, :] = (invs[b] * (dn - low - nrm * tilt)).astype(BF16)

    for t in range(2):
        for half in range(2):
            span = chans // 2
            value = dot(
                dpre_ref[:, half * span : (half + 1) * span], win[t], ((0,), (0,))
            )
            for k in range(span // rows):
                d = half * (span // rows) + k
                term[d % 2, t, (d // 2) % 2, (d // 4) % 2, d // 8] = value[
                    k * rows : (k + 1) * rows, :
                ]

    def send(src, dst, ssem, rsem, peer):
        copy = pltpu.make_async_remote_copy(
            src_ref=src, dst_ref=dst, send_sem=ssem, recv_sem=rsem,
            device_id=(peer,), device_id_type=MESH,
        )
        copy.start()
        return copy

    def input_grad(t):
        value = dot(dpre_ref[...], kern[t], ((1,), (0,)))
        for b in range(clips):
            for l in range(tiles):
                frames32[b, l, pl.ds(t, fpad, stride=2), :] = value[
                    b * fpad : (b + 1) * fpad, l * LANES : (l + 1) * LANES
                ]

    pl.semaphore_wait(barrier, n - 1)

    out0[...] = term[1 - c].astype(BF16)
    copy0 = send(out0, in0, s0, r0, core_peer)
    input_grad(0)
    copy0.wait()
    out1[0] = (term[c, 0, 1 - x] + in0[0, 1 - x].astype(F32)).astype(BF16)
    copy1x = send(out1.at[0], in1.at[0], s1.at[0], r1.at[0], x_peer)
    out1[1] = (term[c, 1, :, 1 - y] + in0[1, :, 1 - y].astype(F32)).astype(BF16)
    copy1y = send(out1.at[1], in1.at[1], s1.at[1], r1.at[1], y_peer)
    input_grad(1)
    copy1x.wait()
    copy1y.wait()
    out2[0] = (
        term[c, 0, x, 1 - y] + in0[0, x, 1 - y].astype(F32) + in1[0, 1 - y].astype(F32)
    ).astype(BF16)
    copy2y = send(out2.at[0], in2.at[0], s2.at[0], r2.at[0], y_peer)
    out2[1] = (
        term[c, 1, 1 - x, y] + in0[1, 1 - x, y].astype(F32) + in1[1, 1 - x].astype(F32)
    ).astype(BF16)
    copy2x = send(out2.at[1], in2.at[1], s2.at[1], r2.at[1], x_peer)
    for b in range(clips):
        for l in range(tiles):
            dinput[b, :, l * LANES : (l + 1) * LANES] = frames32[b, l, 0:frames_in, :].astype(BF16)
    copy2y.wait()
    copy2x.wait()

    def held(t, zz):
        return (
            term[c, t, x, y, zz]
            + in0[t, x, y, zz].astype(F32)
            + in1[t, y if t == 0 else x, zz].astype(F32)
            + in2[t, zz].astype(F32)
        )

    copies3 = []
    for j in range(1, depth):
        zz = (z + j) % depth
        for t in range(2):
            out3[j - 1, t] = held(t, zz).astype(BF16)
        copies3.append(
            send(out3.at[j - 1], in3.at[j - 1], s3.at[j - 1], r3.at[j - 1], (me + 8 * j) % n)
        )
    own = [held(t, z) for t in range(2)]
    for j in range(1, depth):
        copies3[j - 1].wait()
        own = [own[t] + in3[j - 1, t].astype(F32) for t in range(2)]

    squares = own[0] * own[0] + own[1] * own[1]
    fold = sum(squares[:, l * LANES : (l + 1) * LANES] for l in range(tiles))
    fold = sum(fold[k * 8 : (k + 1) * 8, :] for k in range(rows // 8))
    sq_out[...] = fold
    copies = []
    for j in range(1, n):
        copies.append(
            send(sq_out, sq_in.at[j - 1], sq_s.at[j - 1], sq_r.at[j - 1], (me + j) % n)
        )
    for r in range(rows):
        for t in range(2):
            grad[t : t + 1, r * chans : (r + 1) * chans] = own[t][r : r + 1, :]
    for copy in copies:
        copy.wait()
    total = jnp.sum(fold + jnp.sum(sq_in[...], axis=0))
    scale = jnp.minimum(1.0, 1.0 / (jnp.sqrt(jnp.full((1, 1), total)) + 1e-06))

    upd, nm, nf, ns = adamw(grad[...], scale, master[...], first[...], second[...])
    update[...] = upd
    new_master[...] = nm
    new_first[...] = nf
    new_second[...] = ns

    def piece(zz, yy, xx, half=None):
        start = (((zz * 2 + yy) * 2 + xx) * 2 + c) * width
        size = width
        if half is not None:
            size = width // 2
            start = start + half * size
        return gathered.at[:, pl.ds(pl.multiple_of(start, LANES), size)]

    mine = piece(z, y, x)
    mine[...] = nm.astype(BF16)

    pending = []
    arrive = []
    for j in range(1, depth):
        copy = send(mine, mine, zs_s.at[j - 1], zs_r.at[j - 1], (me + 8 * j) % n)
        arrive.append(copy)
    fx, fy = [], []
    for j in range(depth):
        zz = (z + depth - j) % depth
        if j:
            arrive[j - 1].wait()
        block = piece(zz, y, x)
        fx.append(send(block, block, xs.at[j], xr.at[j], x_peer))
        fy.append(send(block, block, ys.at[j], yr.at[j], y_peer))
        pending.append(send(block, block, cs.at[4 * j], cr.at[4 * j], core_peer))
    ex, ey = [], []
    for j in range(depth):
        zz = (z + depth - j) % depth
        fy[j].wait()
        block = piece(zz, 1 - y, x)
        half = piece(zz, 1 - y, x, 0)
        ex.append(send(half, half, dxs.at[j], dxr.at[j], x_peer))
        pending.append(send(block, block, cs.at[4 * j + 1], cr.at[4 * j + 1], core_peer))
        fx[j].wait()
        block = piece(zz, y, 1 - x)
        half = piece(zz, y, 1 - x, 1)
        ey.append(send(half, half, dys.at[j], dyr.at[j], y_peer))
        pending.append(send(block, block, cs.at[4 * j + 2], cr.at[4 * j + 2], core_peer))
    for j in range(depth):
        zz = (z + depth - j) % depth
        ex[j].wait()
        ey[j].wait()
        block = piece(zz, 1 - y, 1 - x)
        pending.append(send(block, block, cs.at[4 * j + 3], cr.at[4 * j + 3], core_peer))
    for copy in pending:
        copy.wait()


def kernel_body(
    n, inputs, weights, ln_gain, ln_bias, projection, targets, master, first_moment, second_moment
):
    clips, frames_in, chans = inputs.shape
    taps = weights.shape[0]
    frames_out = (frames_in - taps) // taps + 1
    width = master.shape[1]
    rows = width // chans
    depth = n // 8
    fpad = -(-(frames_in + 1) // 2 // 8) * 8
    dma = pltpu.SemaphoreType.DMA
    block = (depth, rows, chans)
    piece = jax.ShapeDtypeStruct(master.shape, F32)
    vmem = pl.BlockSpec(memory_space=pltpu.VMEM)
    return pl.pallas_call(
        functools.partial(step_kernel, n, frames_out),
        out_shape=(
            jax.ShapeDtypeStruct(inputs.shape, BF16),
            piece,
            piece,
            piece,
            piece,
            jax.ShapeDtypeStruct(weights.shape, BF16),
        ),
        in_specs=[vmem] * 9,
        out_specs=[vmem] * 6,
        scratch_shapes=[
            pltpu.VMEM((clips, chans // LANES, 2 * fpad, LANES), F32),
            pltpu.VMEM((2, clips * fpad, chans), BF16),
            pltpu.VMEM((clips * fpad, chans), F32),
            pltpu.VMEM((clips * fpad, chans), F32),
            pltpu.VMEM((clips * fpad, chans), BF16),
            pltpu.VMEM((2, 2, 2, 2) + block, F32),
            pltpu.VMEM((2, 2, 2) + block, BF16),
            pltpu.VMEM((2, 2, 2) + block, BF16),
            pltpu.VMEM((2, 2) + block, BF16),
            pltpu.VMEM((2, 2) + block, BF16),
            pltpu.VMEM((2,) + block, BF16),
            pltpu.VMEM((2,) + block, BF16),
            pltpu.VMEM((depth, 2, rows, chans), BF16),
            pltpu.VMEM((depth, 2, rows, chans), BF16),
            pltpu.VMEM((8, LANES), F32),
            pltpu.VMEM((n - 1, 8, LANES), F32),
            pltpu.VMEM(master.shape, F32),
            dma, dma, dma((2,)), dma((2,)), dma((2,)), dma((2,)),
            dma((depth,)), dma((depth,)), dma((n - 1,)), dma((n - 1,)),
            dma((depth,)), dma((depth,)),
            dma((depth,)), dma((depth,)), dma((depth,)), dma((depth,)),
            dma((depth,)), dma((depth,)), dma((depth,)), dma((depth,)),
            dma((4 * depth,)), dma((4 * depth,)),
        ],
        compiler_params=pltpu.CompilerParams(
            collective_id=0, has_side_effects=True, vmem_limit_bytes=50 * 1024 * 1024
        ),
        name="conv_step",
    )(
        inputs, weights.reshape(taps, chans, chans), ln_gain[None], ln_bias[None], projection,
        targets, master, first_moment, second_moment,
    )


def body(n, *args):
    inputs, weights, master = args[0], args[1], args[6]
    chans, width = inputs.shape[2], master.shape[1]
    fits = (
        n % 8 == 0 and n > 8 and weights.shape[0] == 2 and inputs.shape[1] % 2 == 1
        and chans % (2 * LANES) == 0 and width % (16 * chans) == 0
    )
    return kernel_body(n, *args) if fits else plain_body(*args)


def solution(mesh):
    return jax.shard_map(
        functools.partial(body, mesh.shape["dp"]),
        mesh=mesh,
        in_specs=(
            P("dp", None, None),
            P(),
            P(),
            P(),
            P(),
            P("dp", None),
            P(None, "dp"),
            P(None, "dp"),
            P(None, "dp"),
        ),
        out_specs=(
            P("dp", None, None),
            P(None, "dp"),
            P(None, "dp"),
            P(None, "dp"),
            P(None, "dp"),
            P(),
        ),
        check_vma=False,
    )
```

```python
import functools

import jax
import jax.numpy as jnp
from jax import lax
from jax.experimental import pallas as pl
from jax.experimental.pallas import tpu as pltpu
from jax.sharding import PartitionSpec as P

MESH = pl.DeviceIdType.MESH
LANES = 128
F32 = jnp.float32
BF16 = jnp.bfloat16


def norm_act(pre, gain, bias):
    center = pre - jnp.mean(pre, axis=-1, keepdims=True)
    spread = jnp.mean(center * center, axis=-1, keepdims=True)
    normed = center * lax.rsqrt(spread + 1e-05)
    return jax.nn.gelu(normed * gain + bias, approximate=False)


def local_pass(inputs, weights, ln_gain, ln_bias, projection, targets):
    clips, frames_in, chans = inputs.shape
    taps = weights.shape[0]
    frames_out = (frames_in - taps) // taps + 1
    windows = inputs[:, : frames_out * taps].reshape(clips, frames_out, taps, chans)
    kernel = weights.reshape(taps, chans, chans)
    pre = jnp.einsum("bfki,koi->bfo", windows, kernel, preferred_element_type=jnp.float32)
    act, pull = jax.vjp(lambda value: norm_act(value, ln_gain, ln_bias), pre)
    pooled = jnp.mean(act, axis=1).astype(jnp.bfloat16)
    predicted = jnp.dot(pooled, projection, preferred_element_type=jnp.float32)
    miss = (predicted - targets).astype(jnp.bfloat16)
    back = lax.dot_general(
        miss, projection, (((1,), (1,)), ((), ())), preferred_element_type=jnp.float32
    )
    upstream = jnp.broadcast_to(back[:, None, :] / frames_out, act.shape)
    dpre = pull(upstream)[0].astype(jnp.bfloat16)
    dwin = jnp.einsum("bfo,koi->bfki", dpre, kernel, preferred_element_type=jnp.float32).astype(
        jnp.bfloat16
    )
    dinput = dwin.reshape(clips, frames_out * taps, chans)
    tail = jnp.zeros((clips, frames_in - frames_out * taps, chans), jnp.bfloat16)
    return (windows, dpre, jnp.concatenate([dinput, tail], axis=1))


def adamw(grad, scale, master, first_moment, second_moment):
    clipped = scale * grad
    new_first = 0.9 * first_moment + 0.1 * clipped
    new_second = 0.999 * second_moment + 0.001 * clipped * clipped
    update = new_first / (1.0 - 0.9**20) / (jnp.sqrt(new_second / (1.0 - 0.999**20)) + 1e-08)
    new_master = master - 0.0001 * (update + 0.01 * master)
    return update, new_master, new_first, new_second


def plain_body(
    inputs, weights, ln_gain, ln_bias, projection, targets, master, first_moment, second_moment
):
    windows, dpre, input_grad = local_pass(inputs, weights, ln_gain, ln_bias, projection, targets)
    taps = weights.shape[0]
    term = jnp.einsum("bfo,bfki->koi", dpre, windows, preferred_element_type=jnp.float32)
    grad = lax.psum_scatter(term.reshape(taps, -1), "dp", scatter_dimension=1, tiled=True)
    squares = lax.psum(jnp.sum(grad * grad), "dp")
    scale = jnp.minimum(1.0, 1.0 / (jnp.sqrt(squares) + 1e-06))
    update, new_master, new_first, new_second = adamw(
        grad, scale, master, first_moment, second_moment
    )
    new_weights = lax.all_gather(new_master.astype(jnp.bfloat16), "dp", axis=1, tiled=True)
    return (input_grad, update, new_master, new_first, new_second, new_weights)


def dot(a, b, dims):
    return lax.dot_general(a, b, (dims, ((), ())), preferred_element_type=F32)


def step_kernel(
    n, frames_out,
    inputs_hbm, weights_hbm, gain_ref, bias_ref, projection_hbm, targets, master_hbm, first_hbm,
    second_hbm,
    dinput, update, new_master, new_first, new_second, gathered,
    inputs, weights, projection, master, first, second,
    win, kern, pre_ref, slope, dpre_ref, dwin, term,
    out0, in0, out1, in1, out2, in2, out3, in3, sq_out, sq_in, grad,
    load, s0, r0, s1, r1, s2, r2, s3, r3, sq_s, sq_r,
    zs_s, zs_r, xs, xr, ys, yr, dxs, dxr, dys, dyr, cs, cr,
):
    frames_in, clips, chans = inputs.shape
    live_rows = frames_out * clips
    pad_rows = win.shape[0]
    width = grad.shape[1]
    rows = width // chans
    depth = n // 8

    me = lax.axis_index("dp")
    c = me % 2
    x = (me // 2) % 2
    y = (me // 4) % 2
    z = me // 8
    core_peer = me + 1 - 2 * c
    x_peer = me + 2 - 4 * x
    y_peer = me + 4 - 8 * y

    loads = [
        pltpu.make_async_copy(src, dst, load.at[k])
        for k, (src, dst) in enumerate(
            (
                (inputs_hbm, inputs), (weights_hbm, weights), (projection_hbm, projection),
                (master_hbm, master), (first_hbm, first), (second_hbm, second),
            )
        )
    ]
    for copy in loads:
        copy.start()

    barrier = pltpu.get_barrier_semaphore()
    for j in range(1, n):
        pl.semaphore_signal(barrier, inc=1, device_id=((me + j) % n,), device_id_type=MESH)

    loads[0].wait()
    pairs = inputs[0 : 2 * frames_out].reshape(frames_out, 2, clips, chans)
    for t in range(2):
        win[0:live_rows, t * chans : (t + 1) * chans] = (
            pairs[:, t].astype(F32).reshape(live_rows, chans).astype(BF16)
        )
    if pad_rows > live_rows:
        win[live_rows:pad_rows, :] = jnp.zeros((pad_rows - live_rows, 2 * chans), BF16)
    loads[1].wait()
    for q in range(chans // 16):
        flat = weights[:, q * 16 * chans : (q + 1) * 16 * chans].astype(F32)
        flat = flat.reshape(2, 16, chans)
        for t in range(2):
            kern[q * 16 : (q + 1) * 16, t * chans : (t + 1) * chans] = flat[t].astype(BF16)

    pre_ref[...] = dot(win[...], kern[...], ((1,), (1,)))
    gain = gain_ref[...]
    bias = bias_ref[...]
    step = 80 if pad_rows % 80 == 0 else 16
    fold = jnp.zeros((8, chans), F32)
    invs = []
    for base in range(0, pad_rows, step):
        part = slice(base, base + step)
        pre = pre_ref[part, :]
        center = pre - jnp.mean(pre, axis=-1, keepdims=True)
        spread = jnp.mean(center * center, axis=-1, keepdims=True)
        inv = lax.rsqrt(spread + 1e-05)
        nrm = center * inv
        h = nrm * gain + bias
        cdf = 0.5 + 0.5 * lax.erf(h * (0.5**0.5))
        pdf = jnp.exp(-0.5 * h * h) * 0.3989422804014327
        act = h * cdf
        rise = (cdf + h * pdf) * gain
        if base + step > live_rows:
            live = lax.broadcasted_iota(jnp.int32, (step, 1), 0) < live_rows - base
            act = jnp.where(live, act, 0.0)
            rise = jnp.where(live, rise, 0.0)
        slope[part, :] = rise
        pre_ref[part, :] = nrm
        fold = fold + jnp.sum(act.reshape(step // 8, 8, chans), axis=0)
        invs.append(inv)
    pooled = fold
    for k in range(1, 8 // clips):
        pooled = pooled + pltpu.roll(fold, k * clips, 0)
    pooled = (pooled / frames_out).astype(BF16)
    loads[2].wait()
    predicted = dot(pooled, projection[...], ((1,), (0,)))
    goal = jnp.concatenate([targets[...]] * (8 // clips), axis=0)
    miss = (predicted - goal).astype(BF16)
    back = dot(miss, projection[...], ((1,), (1,))) / frames_out
    for k, base in enumerate(range(0, pad_rows, step)):
        part = slice(base, base + step)
        nrm = pre_ref[part, :]
        dn = (slope[part, :].reshape(step // 8, 8, chans) * back[None]).reshape(step, chans)
        low = jnp.mean(dn, axis=-1, keepdims=True)
        tilt = jnp.mean(dn * nrm, axis=-1, keepdims=True)
        dpre_ref[part, :] = (invs[k] * (dn - low - nrm * tilt)).astype(BF16)

    span = chans // 2
    for half in range(2):
        value = dot(dpre_ref[:, half * span : (half + 1) * span], win[...], ((0,), (0,)))
        for k in range(span // rows):
            d = half * (span // rows) + k
            for t in range(2):
                term[d % 2, d // 8, t, (d // 2) % 2, (d // 4) % 2] = value[
                    k * rows : (k + 1) * rows, t * chans : (t + 1) * chans
                ]

    sent = []

    def send(src, dst, ssem, rsem, peer):
        copy = pltpu.make_async_remote_copy(
            src_ref=src, dst_ref=dst, send_sem=ssem, recv_sem=rsem,
            device_id=(peer,), device_id_type=MESH,
        )
        copy.start()
        sent.append(copy)
        return copy

    pl.semaphore_wait(barrier, n - 1)

    order = [(z + j) % depth for j in range(1, depth)] + [z]
    copies0 = []
    for k, zz in enumerate(order):
        out0[zz] = term[1 - c, zz].astype(BF16)
        copies0.append(send(out0.at[zz], in0.at[zz], s0.at[k], r0.at[k], core_peer))
    copies1 = []
    for k, zz in enumerate(order):
        copies0[k].wait_recv()
        out1[zz, 0] = (term[c, zz, 0, 1 - x] + in0[zz, 0, 1 - x].astype(F32)).astype(BF16)
        by_x = send(out1.at[zz, 0], in1.at[zz, 0], s1.at[2 * k], r1.at[2 * k], x_peer)
        out1[zz, 1] = (term[c, zz, 1, :, 1 - y] + in0[zz, 1, :, 1 - y].astype(F32)).astype(BF16)
        by_y = send(out1.at[zz, 1], in1.at[zz, 1], s1.at[2 * k + 1], r1.at[2 * k + 1], y_peer)
        copies1.append((by_x, by_y))
    dwin[...] = dot(dpre_ref[...], kern[...], ((1,), (0,)))

    def held(t, zz):
        return (
            term[c, zz, t, x, y]
            + in0[zz, t, x, y].astype(F32)
            + in1[zz, t, y if t == 0 else x].astype(F32)
            + in2[zz, t].astype(F32)
        )

    copies2, copies3 = [], []

    def to_z(k):
        copies2[k][0].wait_recv()
        copies2[k][1].wait_recv()
        for t in range(2):
            out3[k, t] = held(t, order[k]).astype(BF16)
        copies3.append(
            send(out3.at[k], in3.at[k], s3.at[k], r3.at[k], (me + 8 * (k + 1)) % n)
        )

    for k, zz in enumerate(order):
        copies1[k][0].wait_recv()
        copies1[k][1].wait_recv()
        out2[zz, 0] = (
            term[c, zz, 0, x, 1 - y]
            + in0[zz, 0, x, 1 - y].astype(F32)
            + in1[zz, 0, 1 - y].astype(F32)
        ).astype(BF16)
        by_y = send(out2.at[zz, 0], in2.at[zz, 0], s2.at[2 * k], r2.at[2 * k], y_peer)
        out2[zz, 1] = (
            term[c, zz, 1, 1 - x, y]
            + in0[zz, 1, 1 - x, y].astype(F32)
            + in1[zz, 1, 1 - x].astype(F32)
        ).astype(BF16)
        by_x = send(out2.at[zz, 1], in2.at[zz, 1], s2.at[2 * k + 1], r2.at[2 * k + 1], x_peer)
        copies2.append((by_y, by_x))
        if k:
            to_z(k - 1)
    copies2[-1][0].wait_recv()
    copies2[-1][1].wait_recv()
    own = [held(t, z) for t in range(2)]
    for k in range(depth - 1):
        copies3[k].wait_recv()
        own = [own[t] + in3[k, t].astype(F32) for t in range(2)]

    squares = own[0] * own[0] + own[1] * own[1]
    fold = sum(squares[:, l * LANES : (l + 1) * LANES] for l in range(chans // LANES))
    fold = sum(fold[k * 8 : (k + 1) * 8, :] for k in range(rows // 8))
    sq_out[...] = fold
    norms = []
    for j in range(1, n):
        norms.append(
            send(sq_out, sq_in.at[j - 1], sq_s.at[j - 1], sq_r.at[j - 1], (me + j) % n)
        )
    for r in range(rows):
        for t in range(2):
            grad[t : t + 1, r * chans : (r + 1) * chans] = own[t][r : r + 1, :]
    for k in range(3, 6):
        loads[k].wait()
    taps = [
        dwin[0:live_rows, t * chans : (t + 1) * chans]
        .astype(BF16)
        .reshape(frames_out, 1, clips, chans)
        for t in range(2)
    ]
    dinput[0 : 2 * frames_out] = jnp.concatenate(taps, axis=1).reshape(
        2 * frames_out, clips, chans
    )
    if frames_in > 2 * frames_out:
        dinput[2 * frames_out : frames_in] = jnp.zeros(
            (frames_in - 2 * frames_out, clips, chans), BF16
        )
    for copy in norms:
        copy.wait_recv()
    total = jnp.sum(fold + jnp.sum(sq_in[...], axis=0))
    scale = jnp.minimum(1.0, 1.0 / (jnp.sqrt(jnp.full((1, 1), total)) + 1e-06))

    upd, nm, nf, ns = adamw(grad[...], scale, master[...], first[...], second[...])

    def piece(zz, yy, xx, half=None):
        start = (((zz * 2 + yy) * 2 + xx) * 2 + c) * width
        size = width
        if half is not None:
            size = width // 2
            start = start + half * size
        return gathered.at[:, pl.ds(pl.multiple_of(start, LANES), size)]

    mine = piece(z, y, x)
    mine[...] = nm.astype(BF16)

    arrive = []
    for j in range(1, depth):
        copy = send(mine, mine, zs_s.at[j - 1], zs_r.at[j - 1], (me + 8 * j) % n)
        arrive.append(copy)
    fx, fy, cores = [], [], []
    for j in range(depth):
        zz = (z + depth - j) % depth
        if j:
            arrive[j - 1].wait_recv()
        block = piece(zz, y, x)
        fx.append(send(block, block, xs.at[j], xr.at[j], x_peer))
        fy.append(send(block, block, ys.at[j], yr.at[j], y_peer))
        cores.append(send(block, block, cs.at[4 * j], cr.at[4 * j], core_peer))
        if j == 0:
            update[...] = upd
            new_master[...] = nm
            new_first[...] = nf
            new_second[...] = ns
    ex, ey = [], []
    for j in range(depth):
        zz = (z + depth - j) % depth
        fy[j].wait_recv()
        block = piece(zz, 1 - y, x)
        half = piece(zz, 1 - y, x, 0)
        ex.append(send(half, half, dxs.at[j], dxr.at[j], x_peer))
        cores.append(send(block, block, cs.at[4 * j + 1], cr.at[4 * j + 1], core_peer))
        fx[j].wait_recv()
        block = piece(zz, y, 1 - x)
        half = piece(zz, y, 1 - x, 1)
        ey.append(send(half, half, dys.at[j], dyr.at[j], y_peer))
        cores.append(send(block, block, cs.at[4 * j + 2], cr.at[4 * j + 2], core_peer))
    for j in range(depth):
        zz = (z + depth - j) % depth
        ex[j].wait_recv()
        ey[j].wait_recv()
        block = piece(zz, 1 - y, 1 - x)
        cores.append(send(block, block, cs.at[4 * j + 3], cr.at[4 * j + 3], core_peer))
    for copy in cores:
        copy.wait_recv()
    for copy in sent:
        copy.wait_send()


def hand_over(*refs):
    count = (len(refs) - 1) // 2
    sems = refs[-1]
    copies = [
        pltpu.make_async_copy(refs[k], refs[count + k], sems.at[k]) for k in range(count)
    ]
    for copy in copies:
        copy.start()
    for copy in copies:
        copy.wait()


def kernel_body(
    n, inputs, weights, ln_gain, ln_bias, projection, targets, master, first_moment, second_moment
):
    clips, frames_in, chans = inputs.shape
    taps = weights.shape[0]
    frames_out = (frames_in - taps) // taps + 1
    width = master.shape[1]
    rows = width // chans
    depth = n // 8
    pad = -(-clips * frames_out // 16) * 16
    dma = pltpu.SemaphoreType.DMA
    block = (rows, chans)
    piece = jax.ShapeDtypeStruct(master.shape, F32)
    frames = jnp.transpose(inputs, (1, 0, 2))
    outs = (
        jax.ShapeDtypeStruct(frames.shape, BF16),
        piece,
        piece,
        piece,
        piece,
        jax.ShapeDtypeStruct(weights.shape, BF16),
    )
    vmem = pl.BlockSpec(memory_space=pltpu.VMEM)
    hbm = pl.BlockSpec(memory_space=pl.ANY)
    results = pl.pallas_call(
        functools.partial(step_kernel, n, frames_out),
        out_shape=outs,
        in_specs=[hbm, hbm, vmem, vmem, hbm, vmem, hbm, hbm, hbm],
        out_specs=[vmem] * 6,
        scratch_shapes=[
            pltpu.VMEM(frames.shape, BF16),
            pltpu.VMEM(weights.shape, BF16),
            pltpu.VMEM(projection.shape, BF16),
            pltpu.VMEM(master.shape, F32),
            pltpu.VMEM(master.shape, F32),
            pltpu.VMEM(master.shape, F32),
            pltpu.VMEM((pad, 2 * chans), BF16),
            pltpu.VMEM((chans, 2 * chans), BF16),
            pltpu.VMEM((pad, chans), F32),
            pltpu.VMEM((pad, chans), F32),
            pltpu.VMEM((pad, chans), BF16),
            pltpu.VMEM((pad, 2 * chans), F32),
            pltpu.VMEM((2, depth, 2, 2, 2) + block, F32),
            pltpu.VMEM((depth, 2, 2, 2) + block, BF16),
            pltpu.VMEM((depth, 2, 2, 2) + block, BF16),
            pltpu.VMEM((depth, 2, 2) + block, BF16),
            pltpu.VMEM((depth, 2, 2) + block, BF16),
            pltpu.VMEM((depth, 2) + block, BF16),
            pltpu.VMEM((depth, 2) + block, BF16),
            pltpu.VMEM((depth, 2) + block, BF16),
            pltpu.VMEM((depth, 2) + block, BF16),
            pltpu.VMEM((8, LANES), F32),
            pltpu.VMEM((n - 1, 8, LANES), F32),
            pltpu.VMEM(master.shape, F32),
            dma((6,)),
            dma((depth,)), dma((depth,)),
            dma((2 * depth,)), dma((2 * depth,)),
            dma((2 * depth,)), dma((2 * depth,)),
            dma((depth,)), dma((depth,)), dma((n - 1,)), dma((n - 1,)),
            dma((depth,)), dma((depth,)),
            dma((depth,)), dma((depth,)), dma((depth,)), dma((depth,)),
            dma((depth,)), dma((depth,)), dma((depth,)), dma((depth,)),
            dma((4 * depth,)), dma((4 * depth,)),
        ],
        compiler_params=pltpu.CompilerParams(
            collective_id=0, has_side_effects=True, vmem_limit_bytes=40 * 1024 * 1024
        ),
        name="conv_step",
    )(
        frames, weights, ln_gain[None], ln_bias[None], projection, targets, master, first_moment,
        second_moment,
    )
    results = pl.pallas_call(
        hand_over,
        out_shape=outs,
        in_specs=[hbm] * 6,
        out_specs=[hbm] * 6,
        scratch_shapes=[dma((6,))],
        name="hand_over",
    )(*results)
    return (jnp.transpose(results[0], (1, 0, 2)),) + tuple(results[1:])


def body(n, *args):
    inputs, weights, master = args[0], args[1], args[6]
    chans, width = inputs.shape[2], master.shape[1]
    fits = (
        n % 8 == 0 and n > 8 and weights.shape[0] == 2 and 8 % inputs.shape[0] == 0
        and chans % (2 * LANES) == 0 and width % (16 * chans) == 0
    )
    return kernel_body(n, *args) if fits else plain_body(*args)


def solution(mesh):
    return jax.shard_map(
        functools.partial(body, mesh.shape["dp"]),
        mesh=mesh,
        in_specs=(
            P("dp", None, None),
            P(),
            P(),
            P(),
            P(),
            P("dp", None),
            P(None, "dp"),
            P(None, "dp"),
            P(None, "dp"),
        ),
        out_specs=(
            P("dp", None, None),
            P(None, "dp"),
            P(None, "dp"),
            P(None, "dp"),
            P(None, "dp"),
            P(),
        ),
        check_vma=False,
    )
```

```python
import functools

import jax
import jax.numpy as jnp
from jax import lax
from jax.experimental import pallas as pl
from jax.experimental.pallas import tpu as pltpu
from jax.sharding import PartitionSpec as P

MESH = pl.DeviceIdType.MESH
LANES = 128
F32 = jnp.float32
BF16 = jnp.bfloat16


def norm_act(pre, gain, bias):
    center = pre - jnp.mean(pre, axis=-1, keepdims=True)
    spread = jnp.mean(center * center, axis=-1, keepdims=True)
    normed = center * lax.rsqrt(spread + 1e-05)
    return jax.nn.gelu(normed * gain + bias, approximate=False)


def local_pass(inputs, weights, ln_gain, ln_bias, projection, targets):
    clips, frames_in, chans = inputs.shape
    taps = weights.shape[0]
    frames_out = (frames_in - taps) // taps + 1
    windows = inputs[:, : frames_out * taps].reshape(clips, frames_out, taps, chans)
    kernel = weights.reshape(taps, chans, chans)
    pre = jnp.einsum("bfki,koi->bfo", windows, kernel, preferred_element_type=jnp.float32)
    act, pull = jax.vjp(lambda value: norm_act(value, ln_gain, ln_bias), pre)
    pooled = jnp.mean(act, axis=1).astype(jnp.bfloat16)
    predicted = jnp.dot(pooled, projection, preferred_element_type=jnp.float32)
    miss = (predicted - targets).astype(jnp.bfloat16)
    back = lax.dot_general(
        miss, projection, (((1,), (1,)), ((), ())), preferred_element_type=jnp.float32
    )
    upstream = jnp.broadcast_to(back[:, None, :] / frames_out, act.shape)
    dpre = pull(upstream)[0].astype(jnp.bfloat16)
    dwin = jnp.einsum("bfo,koi->bfki", dpre, kernel, preferred_element_type=jnp.float32).astype(
        jnp.bfloat16
    )
    dinput = dwin.reshape(clips, frames_out * taps, chans)
    tail = jnp.zeros((clips, frames_in - frames_out * taps, chans), jnp.bfloat16)
    return (windows, dpre, jnp.concatenate([dinput, tail], axis=1))


def adamw(grad, scale, master, first_moment, second_moment):
    clipped = scale * grad
    new_first = 0.9 * first_moment + 0.1 * clipped
    new_second = 0.999 * second_moment + 0.001 * clipped * clipped
    update = new_first / (1.0 - 0.9**20) / (jnp.sqrt(new_second / (1.0 - 0.999**20)) + 1e-08)
    new_master = master - 0.0001 * (update + 0.01 * master)
    return update, new_master, new_first, new_second


def plain_body(
    inputs, weights, ln_gain, ln_bias, projection, targets, master, first_moment, second_moment
):
    windows, dpre, input_grad = local_pass(inputs, weights, ln_gain, ln_bias, projection, targets)
    taps = weights.shape[0]
    term = jnp.einsum("bfo,bfki->koi", dpre, windows, preferred_element_type=jnp.float32)
    grad = lax.psum_scatter(term.reshape(taps, -1), "dp", scatter_dimension=1, tiled=True)
    squares = lax.psum(jnp.sum(grad * grad), "dp")
    scale = jnp.minimum(1.0, 1.0 / (jnp.sqrt(squares) + 1e-06))
    update, new_master, new_first, new_second = adamw(
        grad, scale, master, first_moment, second_moment
    )
    new_weights = lax.all_gather(new_master.astype(jnp.bfloat16), "dp", axis=1, tiled=True)
    return (input_grad, update, new_master, new_first, new_second, new_weights)


def dot(a, b, dims):
    return lax.dot_general(a, b, (dims, ((), ())), preferred_element_type=F32)


def step_kernel(
    n, frames_out,
    inputs_hbm, weights_hbm, gain_hbm, bias_hbm, projection_hbm, targets_hbm, master_hbm,
    first_hbm, second_hbm,
    dinput, update, new_master, new_first, new_second, gathered,
    inputs, weights, gain_ref, bias_ref, projection, targets, master, first, second,
    win, kern, pre_ref, slope, dpre_ref, dwin, term,
    out0, in0, out1, in1, out2, in2, out3, in3, sq_out, sq_in, grad,
    load, s0, r0, s1, r1, s2, r2, s3, r3, sq_s, sq_r,
    zs_s, zs_r, xs, xr, ys, yr, dxs, dxr, dys, dyr, cs, cr,
):
    frames_in, clips, chans = inputs.shape
    live_rows = frames_out * clips
    pad_rows = win.shape[0]
    width = grad.shape[1]
    rows = width // chans
    depth = n // 8

    me = lax.axis_index("dp")
    c = me % 2
    x = (me // 2) % 2
    y = (me // 4) % 2
    z = me // 8
    core_peer = me + 1 - 2 * c
    x_peer = me + 2 - 4 * x
    y_peer = me + 4 - 8 * y

    loads = [
        pltpu.make_async_copy(src, dst, load.at[k])
        for k, (src, dst) in enumerate(
            (
                (inputs_hbm, inputs), (weights_hbm, weights), (gain_hbm, gain_ref),
                (bias_hbm, bias_ref), (projection_hbm, projection), (targets_hbm, targets),
                (master_hbm, master), (first_hbm, first), (second_hbm, second),
            )
        )
    ]
    for copy in loads:
        copy.start()

    barrier = pltpu.get_barrier_semaphore()
    for j in range(1, n):
        pl.semaphore_signal(barrier, inc=1, device_id=((me + j) % n,), device_id_type=MESH)

    loads[0].wait()
    pairs = inputs[0 : 2 * frames_out].reshape(frames_out, 2, clips, chans)
    for t in range(2):
        win[0:live_rows, t * chans : (t + 1) * chans] = (
            pairs[:, t].astype(F32).reshape(live_rows, chans).astype(BF16)
        )
    if pad_rows > live_rows:
        win[live_rows:pad_rows, :] = jnp.zeros((pad_rows - live_rows, 2 * chans), BF16)
    loads[1].wait()
    group = 64 if chans % 64 == 0 else 16

    @pl.loop(0, chans // group)
    def _(q):
        lanes = pl.ds(pl.multiple_of(q * group * chans, LANES), group * chans)
        flat = weights[:, lanes].astype(F32).reshape(2, group, chans)
        out = pl.ds(pl.multiple_of(q * group, group), group)
        for t in range(2):
            kern[out, t * chans : (t + 1) * chans] = flat[t].astype(BF16)

    pre_ref[...] = dot(win[...], kern[...], ((1,), (1,)))
    loads[2].wait()
    loads[3].wait()
    gain = gain_ref[...]
    bias = bias_ref[...]
    step = 80 if pad_rows % 80 == 0 else 16

    def forward(i, fold):
        base = pl.multiple_of(i * step, 16)
        part = pl.ds(base, step)
        pre = pre_ref[part, :]
        center = pre - jnp.mean(pre, axis=-1, keepdims=True)
        spread = jnp.mean(center * center, axis=-1, keepdims=True)
        inv = lax.rsqrt(spread + 1e-05)
        nrm = center * inv
        h = nrm * gain + bias
        cdf = 0.5 + 0.5 * lax.erf(h * (0.5**0.5))
        pdf = jnp.exp(-0.5 * h * h) * 0.3989422804014327
        live = lax.broadcasted_iota(jnp.int32, (step, 1), 0) < live_rows - base
        act = jnp.where(live, h * cdf, 0.0)
        slope[part, :] = (cdf + h * pdf) * (gain * jnp.where(live, inv, 0.0))
        pre_ref[part, :] = nrm
        return fold + jnp.sum(act.reshape(step // 8, 8, chans), axis=0)

    fold = lax.fori_loop(0, pad_rows // step, forward, jnp.zeros((8, chans), F32))
    pooled = fold
    for k in range(1, 8 // clips):
        pooled = pooled + pltpu.roll(fold, k * clips, 0)
    pooled = (pooled / frames_out).astype(BF16)
    loads[4].wait()
    loads[5].wait()
    predicted = dot(pooled, projection[...], ((1,), (0,)))
    goal = jnp.concatenate([targets[...]] * (8 // clips), axis=0)
    miss = (predicted - goal).astype(BF16)
    back = dot(miss, projection[...], ((1,), (1,))) / frames_out

    @pl.loop(0, pad_rows // step)
    def _(i):
        part = pl.ds(pl.multiple_of(i * step, 16), step)
        nrm = pre_ref[part, :]
        dn = (slope[part, :].reshape(step // 8, 8, chans) * back[None]).reshape(step, chans)
        low = jnp.mean(dn, axis=-1, keepdims=True)
        tilt = jnp.mean(dn * nrm, axis=-1, keepdims=True)
        dpre_ref[part, :] = (dn - low - nrm * tilt).astype(BF16)

    sent = []

    def send(src, dst, ssem, rsem, peer):
        copy = pltpu.make_async_remote_copy(
            src_ref=src, dst_ref=dst, send_sem=ssem, recv_sem=rsem,
            device_id=(peer,), device_id_type=MESH,
        )
        copy.start()
        sent.append(copy)
        return copy

    order = [(z + j) % depth for j in range(1, depth)] + [z]
    copies0 = []
    copies1 = []

    def to_core(k):
        zz = order[k]
        span = chans // depth
        value = dot(
            dpre_ref[:, pl.ds(pl.multiple_of(zz * span, LANES), span)], win[...], ((0,), (0,))
        )
        for d in range(8):
            for t in range(2):
                term[d % 2, zz, t, (d // 2) % 2, d // 4] = value[
                    d * rows : (d + 1) * rows, t * chans : (t + 1) * chans
                ]
        out0[zz] = term[1 - c, zz].astype(BF16)
        if k == 0:
            pl.semaphore_wait(barrier, n - 1)
        copies0.append(send(out0.at[zz], in0.at[zz], s0.at[k], r0.at[k], core_peer))

    def to_near(k):
        zz = order[k]
        copies0[k].wait_recv()
        out1[zz, 0] = (term[c, zz, 0, 1 - x] + in0[zz, 0, 1 - x].astype(F32)).astype(BF16)
        by_x = send(out1.at[zz, 0], in1.at[zz, 0], s1.at[2 * k], r1.at[2 * k], x_peer)
        out1[zz, 1] = (term[c, zz, 1, :, 1 - y] + in0[zz, 1, :, 1 - y].astype(F32)).astype(BF16)
        by_y = send(out1.at[zz, 1], in1.at[zz, 1], s1.at[2 * k + 1], r1.at[2 * k + 1], y_peer)
        copies1.append((by_x, by_y))

    for k in range(depth):
        to_core(k)
        if k:
            to_near(k - 1)
    to_near(depth - 1)
    dwin[...] = dot(dpre_ref[...], kern[...], ((1,), (0,)))

    def held(t, zz):
        return (
            term[c, zz, t, x, y]
            + in0[zz, t, x, y].astype(F32)
            + in1[zz, t, y if t == 0 else x].astype(F32)
            + in2[zz, t].astype(F32)
        )

    copies2, copies3 = [], []

    def to_z(k):
        copies2[k][0].wait_recv()
        copies2[k][1].wait_recv()
        for t in range(2):
            out3[k, t] = held(t, order[k]).astype(BF16)
        copies3.append(
            send(out3.at[k], in3.at[k], s3.at[k], r3.at[k], (me + 8 * (k + 1)) % n)
        )

    for k, zz in enumerate(order):
        copies1[k][0].wait_recv()
        copies1[k][1].wait_recv()
        out2[zz, 0] = (
            term[c, zz, 0, x, 1 - y]
            + in0[zz, 0, x, 1 - y].astype(F32)
            + in1[zz, 0, 1 - y].astype(F32)
        ).astype(BF16)
        by_y = send(out2.at[zz, 0], in2.at[zz, 0], s2.at[2 * k], r2.at[2 * k], y_peer)
        out2[zz, 1] = (
            term[c, zz, 1, 1 - x, y]
            + in0[zz, 1, 1 - x, y].astype(F32)
            + in1[zz, 1, 1 - x].astype(F32)
        ).astype(BF16)
        by_x = send(out2.at[zz, 1], in2.at[zz, 1], s2.at[2 * k + 1], r2.at[2 * k + 1], x_peer)
        copies2.append((by_y, by_x))
        if k:
            to_z(k - 1)
    copies2[-1][0].wait_recv()
    copies2[-1][1].wait_recv()
    own = [held(t, z) for t in range(2)]
    for k in range(depth - 1):
        copies3[k].wait_recv()
        own = [own[t] + in3[k, t].astype(F32) for t in range(2)]

    squares = own[0] * own[0] + own[1] * own[1]
    fold = sum(squares[:, l * LANES : (l + 1) * LANES] for l in range(chans // LANES))
    fold = sum(fold[k * 8 : (k + 1) * 8, :] for k in range(rows // 8))
    sq_out[...] = fold
    norms = []
    for j in range(1, n):
        norms.append(
            send(sq_out, sq_in.at[j - 1], sq_s.at[j - 1], sq_r.at[j - 1], (me + j) % n)
        )
    for r in range(rows):
        for t in range(2):
            grad[t : t + 1, r * chans : (r + 1) * chans] = own[t][r : r + 1, :]
    for k in range(6, 9):
        loads[k].wait()
    taps = [
        dwin[0:live_rows, t * chans : (t + 1) * chans]
        .astype(BF16)
        .reshape(frames_out, 1, clips, chans)
        for t in range(2)
    ]
    dinput[0 : 2 * frames_out] = jnp.concatenate(taps, axis=1).reshape(
        2 * frames_out, clips, chans
    )
    if frames_in > 2 * frames_out:
        dinput[2 * frames_out : frames_in] = jnp.zeros(
            (frames_in - 2 * frames_out, clips, chans), BF16
        )
    for copy in norms:
        copy.wait_recv()
    total = jnp.sum(fold + jnp.sum(sq_in[...], axis=0))
    scale = jnp.minimum(1.0, 1.0 / (jnp.sqrt(jnp.full((1, 1), total)) + 1e-06))

    upd, nm, nf, ns = adamw(grad[...], scale, master[...], first[...], second[...])

    def piece(zz, yy, xx, half=None):
        start = (((zz * 2 + yy) * 2 + xx) * 2 + c) * width
        size = width
        if half is not None:
            size = width // 2
            start = start + half * size
        return gathered.at[:, pl.ds(pl.multiple_of(start, LANES), size)]

    mine = piece(z, y, x)
    mine[...] = nm.astype(BF16)

    arrive = []
    for j in range(1, depth):
        copy = send(mine, mine, zs_s.at[j - 1], zs_r.at[j - 1], (me + 8 * j) % n)
        arrive.append(copy)
    fx, fy, cores = [], [], []
    for j in range(depth):
        zz = (z + depth - j) % depth
        if j:
            arrive[j - 1].wait_recv()
        block = piece(zz, y, x)
        fx.append(send(block, block, xs.at[j], xr.at[j], x_peer))
        fy.append(send(block, block, ys.at[j], yr.at[j], y_peer))
        cores.append(send(block, block, cs.at[4 * j], cr.at[4 * j], core_peer))
        if j == 0:
            update[...] = upd
            new_master[...] = nm
            new_first[...] = nf
            new_second[...] = ns
    ex, ey = [], []
    for j in range(depth):
        zz = (z + depth - j) % depth
        fy[j].wait_recv()
        block = piece(zz, 1 - y, x)
        half = piece(zz, 1 - y, x, 0)
        ex.append(send(half, half, dxs.at[j], dxr.at[j], x_peer))
        cores.append(send(block, block, cs.at[4 * j + 1], cr.at[4 * j + 1], core_peer))
        fx[j].wait_recv()
        block = piece(zz, y, 1 - x)
        half = piece(zz, y, 1 - x, 1)
        ey.append(send(half, half, dys.at[j], dyr.at[j], y_peer))
        cores.append(send(block, block, cs.at[4 * j + 2], cr.at[4 * j + 2], core_peer))
    for j in range(depth):
        zz = (z + depth - j) % depth
        ex[j].wait_recv()
        ey[j].wait_recv()
        block = piece(zz, 1 - y, 1 - x)
        cores.append(send(block, block, cs.at[4 * j + 3], cr.at[4 * j + 3], core_peer))
    for copy in cores:
        copy.wait_recv()
    for copy in sent:
        copy.wait_send()


def hand_over(*refs):
    count = (len(refs) - 1) // 2
    sems = refs[-1]
    copies = [
        pltpu.make_async_copy(refs[k], refs[count + k], sems.at[k]) for k in range(count)
    ]
    for copy in copies:
        copy.start()
    for copy in copies:
        copy.wait()


def kernel_body(
    n, inputs, weights, ln_gain, ln_bias, projection, targets, master, first_moment, second_moment
):
    clips, frames_in, chans = inputs.shape
    taps = weights.shape[0]
    frames_out = (frames_in - taps) // taps + 1
    width = master.shape[1]
    rows = width // chans
    depth = n // 8
    pad = -(-clips * frames_out // 16) * 16
    dma = pltpu.SemaphoreType.DMA
    block = (rows, chans)
    piece = jax.ShapeDtypeStruct(master.shape, F32)
    frames = jnp.transpose(inputs, (1, 0, 2))
    outs = (
        jax.ShapeDtypeStruct(frames.shape, BF16),
        piece,
        piece,
        piece,
        piece,
        jax.ShapeDtypeStruct(weights.shape, BF16),
    )
    pin = lambda array: pltpu.with_memory_space_constraint(array, pltpu.HBM)
    vmem = pl.BlockSpec(memory_space=pltpu.VMEM)
    hbm = pl.BlockSpec(memory_space=pltpu.HBM)
    results = pl.pallas_call(
        functools.partial(step_kernel, n, frames_out),
        out_shape=outs,
        in_specs=[hbm] * 9,
        out_specs=[vmem] * 6,
        scratch_shapes=[
            pltpu.VMEM(frames.shape, BF16),
            pltpu.VMEM(weights.shape, BF16),
            pltpu.VMEM((1, chans), F32),
            pltpu.VMEM((1, chans), F32),
            pltpu.VMEM(projection.shape, BF16),
            pltpu.VMEM(targets.shape, F32),
            pltpu.VMEM(master.shape, F32),
            pltpu.VMEM(master.shape, F32),
            pltpu.VMEM(master.shape, F32),
            pltpu.VMEM((pad, 2 * chans), BF16),
            pltpu.VMEM((chans, 2 * chans), BF16),
            pltpu.VMEM((pad, chans), F32),
            pltpu.VMEM((pad, chans), F32),
            pltpu.VMEM((pad, chans), BF16),
            pltpu.VMEM((pad, 2 * chans), F32),
            pltpu.VMEM((2, depth, 2, 2, 2) + block, F32),
            pltpu.VMEM((depth, 2, 2, 2) + block, BF16),
            pltpu.VMEM((depth, 2, 2, 2) + block, BF16),
            pltpu.VMEM((depth, 2, 2) + block, BF16),
            pltpu.VMEM((depth, 2, 2) + block, BF16),
            pltpu.VMEM((depth, 2) + block, BF16),
            pltpu.VMEM((depth, 2) + block, BF16),
            pltpu.VMEM((depth, 2) + block, BF16),
            pltpu.VMEM((depth, 2) + block, BF16),
            pltpu.VMEM((8, LANES), F32),
            pltpu.VMEM((n - 1, 8, LANES), F32),
            pltpu.VMEM(master.shape, F32),
            dma((9,)),
            dma((depth,)), dma((depth,)),
            dma((2 * depth,)), dma((2 * depth,)),
            dma((2 * depth,)), dma((2 * depth,)),
            dma((depth,)), dma((depth,)), dma((n - 1,)), dma((n - 1,)),
            dma((depth,)), dma((depth,)),
            dma((depth,)), dma((depth,)), dma((depth,)), dma((depth,)),
            dma((depth,)), dma((depth,)), dma((depth,)), dma((depth,)),
            dma((4 * depth,)), dma((4 * depth,)),
        ],
        compiler_params=pltpu.CompilerParams(
            collective_id=0, has_side_effects=True, vmem_limit_bytes=40 * 1024 * 1024
        ),
        name="conv_step",
    )(
        *map(
            pin,
            (
                frames, weights, ln_gain[None], ln_bias[None], projection, targets, master,
                first_moment, second_moment,
            ),
        )
    )
    results = pl.pallas_call(
        hand_over,
        out_shape=outs,
        in_specs=[vmem] * 6,
        out_specs=[hbm] * 6,
        scratch_shapes=[dma((6,))],
        name="hand_over",
    )(*results)
    return (jnp.transpose(results[0], (1, 0, 2)),) + tuple(results[1:])


def body(n, *args):
    inputs, weights, master = args[0], args[1], args[6]
    chans, width = inputs.shape[2], master.shape[1]
    fits = (
        n % 8 == 0 and n > 8 and weights.shape[0] == 2 and 8 % inputs.shape[0] == 0
        and chans % (2 * LANES) == 0 and width % (16 * chans) == 0
        and chans % (LANES * (n // 8)) == 0
    )
    return kernel_body(n, *args) if fits else plain_body(*args)


def solution(mesh):
    return jax.shard_map(
        functools.partial(body, mesh.shape["dp"]),
        mesh=mesh,
        in_specs=(
            P("dp", None, None),
            P(),
            P(),
            P(),
            P(),
            P("dp", None),
            P(None, "dp"),
            P(None, "dp"),
            P(None, "dp"),
        ),
        out_specs=(
            P("dp", None, None),
            P(None, "dp"),
            P(None, "dp"),
            P(None, "dp"),
            P(None, "dp"),
            P(),
        ),
        check_vma=False,
    )
```

```python
import functools

import jax
import jax.numpy as jnp
from jax import lax
from jax.experimental import pallas as pl
from jax.experimental.pallas import tpu as pltpu
from jax.sharding import PartitionSpec as P

MESH = pl.DeviceIdType.MESH
LANES = 128
F32 = jnp.float32
BF16 = jnp.bfloat16


def norm_act(pre, gain, bias):
    center = pre - jnp.mean(pre, axis=-1, keepdims=True)
    spread = jnp.mean(center * center, axis=-1, keepdims=True)
    normed = center * lax.rsqrt(spread + 1e-05)
    return jax.nn.gelu(normed * gain + bias, approximate=False)


def local_pass(inputs, weights, ln_gain, ln_bias, projection, targets):
    clips, frames_in, chans = inputs.shape
    taps = weights.shape[0]
    frames_out = (frames_in - taps) // taps + 1
    windows = inputs[:, : frames_out * taps].reshape(clips, frames_out, taps, chans)
    kernel = weights.reshape(taps, chans, chans)
    pre = jnp.einsum("bfki,koi->bfo", windows, kernel, preferred_element_type=jnp.float32)
    act, pull = jax.vjp(lambda value: norm_act(value, ln_gain, ln_bias), pre)
    pooled = jnp.mean(act, axis=1).astype(jnp.bfloat16)
    predicted = jnp.dot(pooled, projection, preferred_element_type=jnp.float32)
    miss = (predicted - targets).astype(jnp.bfloat16)
    back = lax.dot_general(
        miss, projection, (((1,), (1,)), ((), ())), preferred_element_type=jnp.float32
    )
    upstream = jnp.broadcast_to(back[:, None, :] / frames_out, act.shape)
    dpre = pull(upstream)[0].astype(jnp.bfloat16)
    dwin = jnp.einsum("bfo,koi->bfki", dpre, kernel, preferred_element_type=jnp.float32).astype(
        jnp.bfloat16
    )
    dinput = dwin.reshape(clips, frames_out * taps, chans)
    tail = jnp.zeros((clips, frames_in - frames_out * taps, chans), jnp.bfloat16)
    return (windows, dpre, jnp.concatenate([dinput, tail], axis=1))


def adamw(grad, scale, master, first_moment, second_moment):
    clipped = scale * grad
    new_first = 0.9 * first_moment + 0.1 * clipped
    new_second = 0.999 * second_moment + 0.001 * clipped * clipped
    update = new_first / (1.0 - 0.9**20) / (jnp.sqrt(new_second / (1.0 - 0.999**20)) + 1e-08)
    new_master = master - 0.0001 * (update + 0.01 * master)
    return update, new_master, new_first, new_second


def plain_body(
    inputs, weights, ln_gain, ln_bias, projection, targets, master, first_moment, second_moment
):
    windows, dpre, input_grad = local_pass(inputs, weights, ln_gain, ln_bias, projection, targets)
    taps = weights.shape[0]
    term = jnp.einsum("bfo,bfki->koi", dpre, windows, preferred_element_type=jnp.float32)
    grad = lax.psum_scatter(term.reshape(taps, -1), "dp", scatter_dimension=1, tiled=True)
    squares = lax.psum(jnp.sum(grad * grad), "dp")
    scale = jnp.minimum(1.0, 1.0 / (jnp.sqrt(squares) + 1e-06))
    update, new_master, new_first, new_second = adamw(
        grad, scale, master, first_moment, second_moment
    )
    new_weights = lax.all_gather(new_master.astype(jnp.bfloat16), "dp", axis=1, tiled=True)
    return (input_grad, update, new_master, new_first, new_second, new_weights)


def dot(a, b, dims):
    return lax.dot_general(a, b, (dims, ((), ())), preferred_element_type=F32)


def step_kernel(
    n, frames_out,
    inputs_hbm, weights_hbm, gain_hbm, bias_hbm, projection_hbm, targets_hbm, master_hbm,
    first_hbm, second_hbm,
    dinput, update, new_master, new_first, new_second, gathered,
    inputs, weights, gain_ref, bias_ref, projection, targets, master, first, second,
    win, kern, pre_ref, slope, dpre_ref, dwin, term,
    out0, in0, out1, in1, out2, in2, out3, in3, sq_out, sq_in, grad,
    load, s0, r0, s1, r1, s2, r2, s3, r3, sq_s, sq_r,
    zs_s, zs_r, xs, xr, ys, yr, dxs, dxr, dys, dyr, cs, cr,
):
    frames_in, clips, chans = inputs.shape
    live_rows = frames_out * clips
    pad_rows = win.shape[0]
    width = grad.shape[1]
    rows = width // chans
    depth = n // 8

    me = lax.axis_index("dp")
    c = me % 2
    x = (me // 2) % 2
    y = (me // 4) % 2
    z = me // 8
    core_peer = me + 1 - 2 * c
    x_peer = me + 2 - 4 * x
    y_peer = me + 4 - 8 * y

    loads = [
        pltpu.make_async_copy(src, dst, load.at[k])
        for k, (src, dst) in enumerate(
            (
                (inputs_hbm, inputs), (weights_hbm, weights), (gain_hbm, gain_ref),
                (bias_hbm, bias_ref), (projection_hbm, projection), (targets_hbm, targets),
                (master_hbm, master), (first_hbm, first), (second_hbm, second),
            )
        )
    ]
    for copy in loads:
        copy.start()

    barrier = pltpu.get_barrier_semaphore()
    for j in range(1, n):
        pl.semaphore_signal(barrier, inc=1, device_id=((me + j) % n,), device_id_type=MESH)

    loads[0].wait()
    pairs = inputs[0 : 2 * frames_out].reshape(frames_out, 2, clips, chans)
    for t in range(2):
        win[0:live_rows, t * chans : (t + 1) * chans] = (
            pairs[:, t].astype(F32).reshape(live_rows, chans).astype(BF16)
        )
    if pad_rows > live_rows:
        win[live_rows:pad_rows, :] = jnp.zeros((pad_rows - live_rows, 2 * chans), BF16)
    loads[1].wait()
    group = 64 if chans % 64 == 0 else 16

    @pl.loop(0, chans // group)
    def _(q):
        lanes = pl.ds(pl.multiple_of(q * group * chans, LANES), group * chans)
        flat = weights[:, lanes].astype(F32).reshape(2, group, chans)
        out = pl.ds(pl.multiple_of(q * group, group), group)
        for t in range(2):
            kern[out, t * chans : (t + 1) * chans] = flat[t].astype(BF16)

    pre_ref[...] = dot(win[...], kern[...], ((1,), (1,)))
    loads[2].wait()
    loads[3].wait()
    gain = gain_ref[...]
    bias = bias_ref[...]
    step = 80 if pad_rows % 80 == 0 else 16

    def forward(i, fold):
        base = pl.multiple_of(i * step, 16)
        part = pl.ds(base, step)
        pre = pre_ref[part, :]
        center = pre - jnp.mean(pre, axis=-1, keepdims=True)
        spread = jnp.mean(center * center, axis=-1, keepdims=True)
        inv = lax.rsqrt(spread + 1e-05)
        nrm = center * inv
        h = nrm * gain + bias
        cdf = 0.5 + 0.5 * lax.erf(h * (0.5**0.5))
        pdf = jnp.exp(-0.5 * h * h) * 0.3989422804014327
        live = lax.broadcasted_iota(jnp.int32, (step, 1), 0) < live_rows - base
        act = jnp.where(live, h * cdf, 0.0)
        slope[part, :] = (cdf + h * pdf) * (gain * jnp.where(live, inv, 0.0))
        pre_ref[part, :] = nrm
        return fold + jnp.sum(act.reshape(step // 8, 8, chans), axis=0)

    fold = lax.fori_loop(0, pad_rows // step, forward, jnp.zeros((8, chans), F32))
    pooled = fold
    for k in range(1, 8 // clips):
        pooled = pooled + pltpu.roll(fold, k * clips, 0)
    pooled = (pooled / frames_out).astype(BF16)
    loads[4].wait()
    loads[5].wait()
    predicted = dot(pooled, projection[...], ((1,), (0,)))
    goal = jnp.concatenate([targets[...]] * (8 // clips), axis=0)
    miss = (predicted - goal).astype(BF16)
    back = dot(miss, projection[...], ((1,), (1,))) / frames_out

    @pl.loop(0, pad_rows // step)
    def _(i):
        part = pl.ds(pl.multiple_of(i * step, 16), step)
        nrm = pre_ref[part, :]
        dn = (slope[part, :].reshape(step // 8, 8, chans) * back[None]).reshape(step, chans)
        low = jnp.mean(dn, axis=-1, keepdims=True)
        tilt = jnp.mean(dn * nrm, axis=-1, keepdims=True)
        dpre_ref[part, :] = (dn - low - nrm * tilt).astype(BF16)

    sent = []

    def send(src, dst, ssem, rsem, peer):
        copy = pltpu.make_async_remote_copy(
            src_ref=src, dst_ref=dst, send_sem=ssem, recv_sem=rsem,
            device_id=(peer,), device_id_type=MESH,
        )
        copy.start()
        sent.append(copy)
        return copy

    order = [(z + j) % depth for j in range(1, depth)] + [z]
    copies0 = []
    copies1 = []

    def to_core(k):
        zz = order[k]
        span = chans // depth
        value = dot(
            dpre_ref[:, pl.ds(pl.multiple_of(zz * span, LANES), span)], win[...], ((0,), (0,))
        )
        for d in range(8):
            for t in range(2):
                term[d % 2, zz, t, (d // 2) % 2, d // 4] = value[
                    d * rows : (d + 1) * rows, t * chans : (t + 1) * chans
                ]
        out0[zz] = term[1 - c, zz].astype(BF16)
        if k == 0:
            pl.semaphore_wait(barrier, n - 1)
        copies0.append(send(out0.at[zz], in0.at[zz], s0.at[k], r0.at[k], core_peer))

    def to_near(k):
        zz = order[k]
        copies0[k].wait_recv()
        out1[zz, 0] = (term[c, zz, 0, 1 - x] + in0[zz, 0, 1 - x].astype(F32)).astype(BF16)
        by_x = send(out1.at[zz, 0], in1.at[zz, 0], s1.at[2 * k], r1.at[2 * k], x_peer)
        out1[zz, 1] = (term[c, zz, 1, :, 1 - y] + in0[zz, 1, :, 1 - y].astype(F32)).astype(BF16)
        by_y = send(out1.at[zz, 1], in1.at[zz, 1], s1.at[2 * k + 1], r1.at[2 * k + 1], y_peer)
        copies1.append((by_x, by_y))

    for k in range(depth):
        to_core(k)
        if k:
            to_near(k - 1)
    to_near(depth - 1)
    dwin[...] = dot(dpre_ref[...], kern[...], ((1,), (0,)))

    def held(t, zz):
        return (
            term[c, zz, t, x, y]
            + in0[zz, t, x, y].astype(F32)
            + in1[zz, t, y if t == 0 else x].astype(F32)
            + in2[zz, t].astype(F32)
        )

    copies2, copies3 = [], []

    def to_z(k):
        copies2[k][0].wait_recv()
        copies2[k][1].wait_recv()
        for t in range(2):
            out3[k, t] = held(t, order[k]).astype(BF16)
        copies3.append(
            send(out3.at[k], in3.at[k], s3.at[k], r3.at[k], (me + 8 * (k + 1)) % n)
        )

    for k, zz in enumerate(order):
        copies1[k][0].wait_recv()
        copies1[k][1].wait_recv()
        out2[zz, 0] = (
            term[c, zz, 0, x, 1 - y]
            + in0[zz, 0, x, 1 - y].astype(F32)
            + in1[zz, 0, 1 - y].astype(F32)
        ).astype(BF16)
        by_y = send(out2.at[zz, 0], in2.at[zz, 0], s2.at[2 * k], r2.at[2 * k], y_peer)
        out2[zz, 1] = (
            term[c, zz, 1, 1 - x, y]
            + in0[zz, 1, 1 - x, y].astype(F32)
            + in1[zz, 1, 1 - x].astype(F32)
        ).astype(BF16)
        by_x = send(out2.at[zz, 1], in2.at[zz, 1], s2.at[2 * k + 1], r2.at[2 * k + 1], x_peer)
        copies2.append((by_y, by_x))
        if k:
            to_z(k - 1)
    copies2[-1][0].wait_recv()
    copies2[-1][1].wait_recv()
    own = [held(t, z) for t in range(2)]
    for k in range(depth - 1):
        copies3[k].wait_recv()
        own = [own[t] + in3[k, t].astype(F32) for t in range(2)]

    squares = own[0] * own[0] + own[1] * own[1]
    fold = sum(squares[:, l * LANES : (l + 1) * LANES] for l in range(chans // LANES))
    sq_out[...] = jnp.sum(fold, axis=0, keepdims=True)
    earlier = tuple(sent)
    sent.clear()
    norms = []
    for j in range(1, n):
        norms.append(
            send(sq_out, sq_in.at[pl.ds(j - 1, 1)], sq_s.at[j - 1], sq_r.at[j - 1], (me + j) % n)
        )
    for r in range(rows):
        for t in range(2):
            grad[t : t + 1, r * chans : (r + 1) * chans] = own[t][r : r + 1, :]
    for k in range(6, 9):
        loads[k].wait()
    taps = [
        dwin[0:live_rows, t * chans : (t + 1) * chans]
        .astype(BF16)
        .reshape(frames_out, 1, clips, chans)
        for t in range(2)
    ]
    dinput[0 : 2 * frames_out] = jnp.concatenate(taps, axis=1).reshape(
        2 * frames_out, clips, chans
    )
    if frames_in > 2 * frames_out:
        dinput[2 * frames_out : frames_in] = jnp.zeros(
            (frames_in - 2 * frames_out, clips, chans), BF16
        )
    for copy in earlier:
        copy.wait_send()
    for copy in norms:
        copy.wait_recv()
    total = jnp.sum(sq_in[...]) + jnp.sum(sq_out[...])
    scale = jnp.minimum(1.0, 1.0 / (jnp.sqrt(jnp.full((1, 1), total)) + 1e-06))

    upd, nm, nf, ns = adamw(grad[...], scale, master[...], first[...], second[...])

    def piece(zz, yy, xx, half=None):
        start = (((zz * 2 + yy) * 2 + xx) * 2 + c) * width
        size = width
        if half is not None:
            size = width // 2
            start = start + half * size
        return gathered.at[:, pl.ds(pl.multiple_of(start, LANES), size)]

    mine = piece(z, y, x)
    mine[...] = nm.astype(BF16)

    arrive = []
    for j in range(1, depth):
        copy = send(mine, mine, zs_s.at[j - 1], zs_r.at[j - 1], (me + 8 * j) % n)
        arrive.append(copy)
    fx, fy, cores = [], [], []
    for j in range(depth):
        zz = (z + depth - j) % depth
        if j:
            arrive[j - 1].wait_recv()
        block = piece(zz, y, x)
        fx.append(send(block, block, xs.at[j], xr.at[j], x_peer))
        fy.append(send(block, block, ys.at[j], yr.at[j], y_peer))
        cores.append(send(block, block, cs.at[4 * j], cr.at[4 * j], core_peer))
        if j == 0:
            update[...] = upd
            new_master[...] = nm
            new_first[...] = nf
            new_second[...] = ns
            for copy in norms:
                copy.wait_send()
                sent.remove(copy)
    ex, ey = [], []
    for j in range(depth):
        zz = (z + depth - j) % depth
        fy[j].wait_recv()
        block = piece(zz, 1 - y, x)
        half = piece(zz, 1 - y, x, 0)
        ex.append(send(half, half, dxs.at[j], dxr.at[j], x_peer))
        cores.append(send(block, block, cs.at[4 * j + 1], cr.at[4 * j + 1], core_peer))
        fx[j].wait_recv()
        block = piece(zz, y, 1 - x)
        half = piece(zz, y, 1 - x, 1)
        ey.append(send(half, half, dys.at[j], dyr.at[j], y_peer))
        cores.append(send(block, block, cs.at[4 * j + 2], cr.at[4 * j + 2], core_peer))
    for j in range(depth):
        zz = (z + depth - j) % depth
        ex[j].wait_recv()
        ey[j].wait_recv()
        block = piece(zz, 1 - y, 1 - x)
        cores.append(send(block, block, cs.at[4 * j + 3], cr.at[4 * j + 3], core_peer))
    for copy in cores:
        copy.wait_recv()
    for copy in sent:
        copy.wait_send()


def hand_over(*refs):
    count = (len(refs) - 1) // 2
    sems = refs[-1]
    copies = [
        pltpu.make_async_copy(refs[k], refs[count + k], sems.at[k]) for k in range(count)
    ]
    for copy in copies:
        copy.start()
    for copy in copies:
        copy.wait()


def kernel_body(
    n, inputs, weights, ln_gain, ln_bias, projection, targets, master, first_moment, second_moment
):
    clips, frames_in, chans = inputs.shape
    taps = weights.shape[0]
    frames_out = (frames_in - taps) // taps + 1
    width = master.shape[1]
    rows = width // chans
    depth = n // 8
    pad = -(-clips * frames_out // 16) * 16
    dma = pltpu.SemaphoreType.DMA
    block = (rows, chans)
    piece = jax.ShapeDtypeStruct(master.shape, F32)
    frames = jnp.transpose(inputs, (1, 0, 2))
    outs = (
        jax.ShapeDtypeStruct(frames.shape, BF16),
        piece,
        piece,
        piece,
        piece,
        jax.ShapeDtypeStruct(weights.shape, BF16),
    )
    pin = lambda array: pltpu.with_memory_space_constraint(array, pltpu.HBM)
    vmem = pl.BlockSpec(memory_space=pltpu.VMEM)
    hbm = pl.BlockSpec(memory_space=pltpu.HBM)
    results = pl.pallas_call(
        functools.partial(step_kernel, n, frames_out),
        out_shape=outs,
        in_specs=[hbm] * 9,
        out_specs=[vmem] * 6,
        scratch_shapes=[
            pltpu.VMEM(frames.shape, BF16),
            pltpu.VMEM(weights.shape, BF16),
            pltpu.VMEM((1, chans), F32),
            pltpu.VMEM((1, chans), F32),
            pltpu.VMEM(projection.shape, BF16),
            pltpu.VMEM(targets.shape, F32),
            pltpu.VMEM(master.shape, F32),
            pltpu.VMEM(master.shape, F32),
            pltpu.VMEM(master.shape, F32),
            pltpu.VMEM((pad, 2 * chans), BF16),
            pltpu.VMEM((chans, 2 * chans), BF16),
            pltpu.VMEM((pad, chans), F32),
            pltpu.VMEM((pad, chans), F32),
            pltpu.VMEM((pad, chans), BF16),
            pltpu.VMEM((pad, 2 * chans), F32),
            pltpu.VMEM((2, depth, 2, 2, 2) + block, F32),
            pltpu.VMEM((depth, 2, 2, 2) + block, BF16),
            pltpu.VMEM((depth, 2, 2, 2) + block, BF16),
            pltpu.VMEM((depth, 2, 2) + block, BF16),
            pltpu.VMEM((depth, 2, 2) + block, BF16),
            pltpu.VMEM((depth, 2) + block, BF16),
            pltpu.VMEM((depth, 2) + block, BF16),
            pltpu.VMEM((depth, 2) + block, BF16),
            pltpu.VMEM((depth, 2) + block, BF16),
            pltpu.VMEM((1, LANES), F32),
            pltpu.VMEM((n - 1, LANES), F32),
            pltpu.VMEM(master.shape, F32),
            dma((9,)),
            dma((depth,)), dma((depth,)),
            dma((2 * depth,)), dma((2 * depth,)),
            dma((2 * depth,)), dma((2 * depth,)),
            dma((depth,)), dma((depth,)), dma((n - 1,)), dma((n - 1,)),
            dma((depth,)), dma((depth,)),
            dma((depth,)), dma((depth,)), dma((depth,)), dma((depth,)),
            dma((depth,)), dma((depth,)), dma((depth,)), dma((depth,)),
            dma((4 * depth,)), dma((4 * depth,)),
        ],
        compiler_params=pltpu.CompilerParams(
            collective_id=0, has_side_effects=True, vmem_limit_bytes=40 * 1024 * 1024
        ),
        name="conv_step",
    )(
        *map(
            pin,
            (
                frames, weights, ln_gain[None], ln_bias[None], projection, targets, master,
                first_moment, second_moment,
            ),
        )
    )
    results = pl.pallas_call(
        hand_over,
        out_shape=outs,
        in_specs=[vmem] * 6,
        out_specs=[hbm] * 6,
        scratch_shapes=[dma((6,))],
        compiler_params=pltpu.CompilerParams(vmem_limit_bytes=2 * 1024 * 1024),
        name="hand_over",
    )(*results)
    return (jnp.transpose(results[0], (1, 0, 2)),) + tuple(results[1:])


def body(n, *args):
    inputs, weights, master = args[0], args[1], args[6]
    chans, width = inputs.shape[2], master.shape[1]
    fits = (
        n % 8 == 0 and n > 8 and weights.shape[0] == 2 and 8 % inputs.shape[0] == 0
        and chans % (2 * LANES) == 0 and width % (16 * chans) == 0
        and chans % (LANES * (n // 8)) == 0
    )
    return kernel_body(n, *args) if fits else plain_body(*args)


def solution(mesh):
    return jax.shard_map(
        functools.partial(body, mesh.shape["dp"]),
        mesh=mesh,
        in_specs=(
            P("dp", None, None),
            P(),
            P(),
            P(),
            P(),
            P("dp", None),
            P(None, "dp"),
            P(None, "dp"),
            P(None, "dp"),
        ),
        out_specs=(
            P("dp", None, None),
            P(None, "dp"),
            P(None, "dp"),
            P(None, "dp"),
            P(None, "dp"),
            P(),
        ),
        check_vma=False,
    )
```

```python
import functools

import jax
import jax.numpy as jnp
from jax import lax
from jax.experimental import pallas as pl
from jax.experimental.pallas import tpu as pltpu
from jax.sharding import PartitionSpec as P

MESH = pl.DeviceIdType.MESH
LANES = 128
F32 = jnp.float32
BF16 = jnp.bfloat16


def norm_act(pre, gain, bias):
    center = pre - jnp.mean(pre, axis=-1, keepdims=True)
    spread = jnp.mean(center * center, axis=-1, keepdims=True)
    normed = center * lax.rsqrt(spread + 1e-05)
    return jax.nn.gelu(normed * gain + bias, approximate=False)


def local_pass(inputs, weights, ln_gain, ln_bias, projection, targets):
    clips, frames_in, chans = inputs.shape
    taps = weights.shape[0]
    frames_out = (frames_in - taps) // taps + 1
    windows = inputs[:, : frames_out * taps].reshape(clips, frames_out, taps, chans)
    kernel = weights.reshape(taps, chans, chans)
    pre = jnp.einsum("bfki,koi->bfo", windows, kernel, preferred_element_type=jnp.float32)
    act, pull = jax.vjp(lambda value: norm_act(value, ln_gain, ln_bias), pre)
    pooled = jnp.mean(act, axis=1).astype(jnp.bfloat16)
    predicted = jnp.dot(pooled, projection, preferred_element_type=jnp.float32)
    miss = (predicted - targets).astype(jnp.bfloat16)
    back = lax.dot_general(
        miss, projection, (((1,), (1,)), ((), ())), preferred_element_type=jnp.float32
    )
    upstream = jnp.broadcast_to(back[:, None, :] / frames_out, act.shape)
    dpre = pull(upstream)[0].astype(jnp.bfloat16)
    dwin = jnp.einsum("bfo,koi->bfki", dpre, kernel, preferred_element_type=jnp.float32).astype(
        jnp.bfloat16
    )
    dinput = dwin.reshape(clips, frames_out * taps, chans)
    tail = jnp.zeros((clips, frames_in - frames_out * taps, chans), jnp.bfloat16)
    return (windows, dpre, jnp.concatenate([dinput, tail], axis=1))


def adamw(grad, scale, master, first_moment, second_moment):
    clipped = scale * grad
    new_first = 0.9 * first_moment + 0.1 * clipped
    new_second = 0.999 * second_moment + 0.001 * clipped * clipped
    update = new_first / (1.0 - 0.9**20) / (jnp.sqrt(new_second / (1.0 - 0.999**20)) + 1e-08)
    new_master = master - 0.0001 * (update + 0.01 * master)
    return update, new_master, new_first, new_second


def plain_body(
    inputs, weights, ln_gain, ln_bias, projection, targets, master, first_moment, second_moment
):
    windows, dpre, input_grad = local_pass(inputs, weights, ln_gain, ln_bias, projection, targets)
    taps = weights.shape[0]
    term = jnp.einsum("bfo,bfki->koi", dpre, windows, preferred_element_type=jnp.float32)
    grad = lax.psum_scatter(term.reshape(taps, -1), "dp", scatter_dimension=1, tiled=True)
    squares = lax.psum(jnp.sum(grad * grad), "dp")
    scale = jnp.minimum(1.0, 1.0 / (jnp.sqrt(squares) + 1e-06))
    update, new_master, new_first, new_second = adamw(
        grad, scale, master, first_moment, second_moment
    )
    new_weights = lax.all_gather(new_master.astype(jnp.bfloat16), "dp", axis=1, tiled=True)
    return (input_grad, update, new_master, new_first, new_second, new_weights)


def dot(a, b, dims):
    return lax.dot_general(a, b, (dims, ((), ())), preferred_element_type=F32)


def step_kernel(
    n, frames_out,
    inputs_hbm, weights_hbm, gain_hbm, bias_hbm, projection_hbm, targets_hbm, master_hbm,
    first_hbm, second_hbm,
    dinput, update, new_master, new_first, new_second, gathered,
    inputs, weights, gain_ref, bias_ref, projection, targets, master, first, second,
    win, kern, pre_ref, slope, dpre_ref, dwin, term,
    out0, in0, out1, in1, out3, in3, sq_out, sq_in, grad,
    load, s0, r0, s1, r1, s3, r3, sq_s, sq_r, zs_s, zs_r, near_s, near_r, cs, cr,
):
    frames_in, clips, chans = inputs.shape
    live_rows = frames_out * clips
    pad_rows = win.shape[0]
    width = grad.shape[1]
    rows = width // chans
    depth = n // 8

    me = lax.axis_index("dp")
    c = me % 2
    x = (me // 2) % 2
    y = (me // 4) % 2
    z = me // 8
    core_peer = me + 1 - 2 * c
    x_peer = me + 2 - 4 * x
    y_peer = me + 4 - 8 * y
    near = (
        (1 - x, 1 - y, x_peer + y_peer - me),
        (1 - x, y, x_peer),
        (x, 1 - y, y_peer),
    )

    loads = [
        pltpu.make_async_copy(src, dst, load.at[k])
        for k, (src, dst) in enumerate(
            (
                (inputs_hbm, inputs), (weights_hbm, weights), (gain_hbm, gain_ref),
                (bias_hbm, bias_ref), (projection_hbm, projection), (targets_hbm, targets),
                (master_hbm, master), (first_hbm, first), (second_hbm, second),
            )
        )
    ]
    for copy in loads:
        copy.start()

    barrier = pltpu.get_barrier_semaphore()
    for j in range(1, n):
        pl.semaphore_signal(barrier, inc=1, device_id=((me + j) % n,), device_id_type=MESH)

    loads[0].wait()
    pairs = inputs[0 : 2 * frames_out].reshape(frames_out, 2, clips, chans)
    for t in range(2):
        win[0:live_rows, t * chans : (t + 1) * chans] = (
            pairs[:, t].reshape(live_rows, chans)
        )
    if pad_rows > live_rows:
        win[live_rows:pad_rows, :] = jnp.zeros((pad_rows - live_rows, 2 * chans), BF16)
    loads[1].wait()
    group = 64 if chans % 64 == 0 else 16

    @pl.loop(0, chans // group)
    def _(q):
        lanes = pl.ds(pl.multiple_of(q * group * chans, LANES), group * chans)
        flat = weights[:, lanes].reshape(2, group, chans)
        out = pl.ds(pl.multiple_of(q * group, group), group)
        for t in range(2):
            kern[out, t * chans : (t + 1) * chans] = flat[t]

    pre_ref[...] = dot(win[...], kern[...], ((1,), (1,)))
    loads[2].wait()
    loads[3].wait()
    gain = gain_ref[...]
    bias = bias_ref[...]
    step = 80 if pad_rows % 80 == 0 else 16

    def forward(i, fold):
        base = pl.multiple_of(i * step, 16)
        part = pl.ds(base, step)
        pre = pre_ref[part, :]
        center = pre - jnp.mean(pre, axis=-1, keepdims=True)
        spread = jnp.mean(center * center, axis=-1, keepdims=True)
        inv = lax.rsqrt(spread + 1e-05)
        nrm = center * inv
        h = nrm * gain + bias
        cdf = 0.5 + 0.5 * lax.erf(h * (0.5**0.5))
        pdf = jnp.exp(-0.5 * h * h) * 0.3989422804014327
        live = lax.broadcasted_iota(jnp.int32, (step, 1), 0) < live_rows - base
        act = jnp.where(live, h * cdf, 0.0)
        slope[part, :] = (cdf + h * pdf) * (gain * jnp.where(live, inv, 0.0))
        pre_ref[part, :] = nrm
        return fold + jnp.sum(act.reshape(step // 8, 8, chans), axis=0)

    fold = lax.fori_loop(0, pad_rows // step, forward, jnp.zeros((8, chans), F32))
    pooled = fold
    for k in range(1, 8 // clips):
        pooled = pooled + pltpu.roll(fold, k * clips, 0)
    pooled = (pooled / frames_out).astype(BF16)
    loads[4].wait()
    loads[5].wait()
    predicted = dot(pooled, projection[...], ((1,), (0,)))
    goal = jnp.concatenate([targets[...]] * (8 // clips), axis=0)
    miss = (predicted - goal).astype(BF16)
    back = dot(miss, projection[...], ((1,), (1,))) / frames_out

    @pl.loop(0, pad_rows // step)
    def _(i):
        part = pl.ds(pl.multiple_of(i * step, 16), step)
        nrm = pre_ref[part, :]
        dn = (slope[part, :].reshape(step // 8, 8, chans) * back[None]).reshape(step, chans)
        low = jnp.mean(dn, axis=-1, keepdims=True)
        tilt = jnp.mean(dn * nrm, axis=-1, keepdims=True)
        dpre_ref[part, :] = (dn - low - nrm * tilt).astype(BF16)

    sent = []

    def send(src, dst, ssem, rsem, peer):
        copy = pltpu.make_async_remote_copy(
            src_ref=src, dst_ref=dst, send_sem=ssem, recv_sem=rsem,
            device_id=(peer,), device_id_type=MESH,
        )
        copy.start()
        sent.append(copy)
        return copy

    order = [(z + j) % depth for j in range(1, depth)] + [z]
    copies0 = []
    copies1 = []

    def to_core(k):
        zz = order[k]
        span = chans // depth
        value = dot(
            dpre_ref[:, pl.ds(pl.multiple_of(zz * span, LANES), span)], win[...], ((0,), (0,))
        )
        for d in range(8):
            for t in range(2):
                term[d % 2, zz, (d // 2) % 2, d // 4, t] = value[
                    d * rows : (d + 1) * rows, t * chans : (t + 1) * chans
                ]
        out0[zz] = term[1 - c, zz].astype(BF16)
        if k == 0:
            pl.semaphore_wait(barrier, n - 1)
        copies0.append(send(out0.at[zz], in0.at[zz], s0.at[k], r0.at[k], core_peer))

    def to_near(k):
        zz = order[k]
        copies0[k].wait_recv()
        group1 = []
        for i, (xx, yy, peer) in enumerate(near):
            out1[zz, i] = (term[c, zz, xx, yy] + in0[zz, xx, yy].astype(F32)).astype(BF16)
            group1.append(
                send(out1.at[zz, i], in1.at[zz, i], s1.at[3 * k + i], r1.at[3 * k + i], peer)
            )
        copies1.append(group1)

    for k in range(depth):
        to_core(k)
        if k:
            to_near(k - 1)
    to_near(depth - 1)
    dwin[...] = dot(dpre_ref[...], kern[...], ((1,), (0,)))

    def held(k):
        zz = order[k]
        for copy in copies1[k]:
            copy.wait_recv()
        value = term[c, zz, x, y] + in0[zz, x, y].astype(F32)
        for i in range(3):
            value = value + in1[zz, i].astype(F32)
        return value

    copies3 = []
    for k in range(depth - 1):
        out3[k] = held(k).astype(BF16)
        copies3.append(
            send(out3.at[k], in3.at[k], s3.at[k], r3.at[k], (me + 8 * (k + 1)) % n)
        )
    own = held(depth - 1)
    for k in range(depth - 1):
        copies3[k].wait_recv()
        own = own + in3[k].astype(F32)

    squares = own[0] * own[0] + own[1] * own[1]
    fold = sum(squares[:, l * LANES : (l + 1) * LANES] for l in range(chans // LANES))
    sq_out[...] = jnp.sum(fold, axis=0, keepdims=True)
    earlier = tuple(sent)
    sent.clear()
    norms = []
    for j in range(1, n):
        norms.append(
            send(sq_out, sq_in.at[pl.ds(j - 1, 1)], sq_s.at[j - 1], sq_r.at[j - 1], (me + j) % n)
        )
    for r in range(rows):
        for t in range(2):
            grad[t : t + 1, r * chans : (r + 1) * chans] = own[t][r : r + 1, :]
    for k in range(6, 9):
        loads[k].wait()
    taps = [
        dwin[0:live_rows, t * chans : (t + 1) * chans]
        .astype(BF16)
        .reshape(frames_out, 1, clips, chans)
        for t in range(2)
    ]
    dinput[0 : 2 * frames_out] = jnp.concatenate(taps, axis=1).reshape(
        2 * frames_out, clips, chans
    )
    if frames_in > 2 * frames_out:
        dinput[2 * frames_out : frames_in] = jnp.zeros(
            (frames_in - 2 * frames_out, clips, chans), BF16
        )
    for copy in earlier:
        copy.wait_send()
    for copy in norms:
        copy.wait_recv()
    total = jnp.sum(sq_in[...]) + jnp.sum(sq_out[...])
    scale = jnp.minimum(1.0, 1.0 / (jnp.sqrt(jnp.full((1, 1), total)) + 1e-06))

    upd, nm, nf, ns = adamw(grad[...], scale, master[...], first[...], second[...])

    def piece(zz, yy, xx):
        start = (((zz * 2 + yy) * 2 + xx) * 2 + c) * width
        return gathered.at[:, pl.ds(pl.multiple_of(start, LANES), width)]

    mine = piece(z, y, x)
    mine[...] = nm.astype(BF16)

    arrive = []
    for j in range(1, depth):
        copy = send(mine, mine, zs_s.at[j - 1], zs_r.at[j - 1], (me + 8 * j) % n)
        arrive.append(copy)
    around, cores = [], []
    for j in range(depth):
        zz = (z + depth - j) % depth
        if j:
            arrive[j - 1].wait_recv()
        block = piece(zz, y, x)
        group1 = []
        for i, (xx, yy, peer) in enumerate(near):
            group1.append(send(block, block, near_s.at[3 * j + i], near_r.at[3 * j + i], peer))
        around.append(group1)
        cores.append(send(block, block, cs.at[4 * j + 3], cr.at[4 * j + 3], core_peer))
        if j == 0:
            update[...] = upd
            new_master[...] = nm
            new_first[...] = nf
            new_second[...] = ns
            for copy in norms:
                copy.wait_send()
                sent.remove(copy)
    for j in range(depth):
        zz = (z + depth - j) % depth
        for i in (1, 2, 0):
            around[j][i].wait_recv()
            block = piece(zz, near[i][1], near[i][0])
            cores.append(send(block, block, cs.at[4 * j + i], cr.at[4 * j + i], core_peer))
    for copy in cores:
        copy.wait_recv()
    for copy in sent:
        copy.wait_send()


def hand_over(*refs):
    count = (len(refs) - 1) // 2
    sems = refs[-1]
    copies = [
        pltpu.make_async_copy(refs[k], refs[count + k], sems.at[k]) for k in range(count)
    ]
    for copy in copies:
        copy.start()
    for copy in copies:
        copy.wait()


def kernel_body(
    n, inputs, weights, ln_gain, ln_bias, projection, targets, master, first_moment, second_moment
):
    clips, frames_in, chans = inputs.shape
    taps = weights.shape[0]
    frames_out = (frames_in - taps) // taps + 1
    width = master.shape[1]
    rows = width // chans
    depth = n // 8
    pad = -(-clips * frames_out // 16) * 16
    dma = pltpu.SemaphoreType.DMA
    block = (rows, chans)
    piece = jax.ShapeDtypeStruct(master.shape, F32)
    frames = jnp.transpose(inputs, (1, 0, 2))
    outs = (
        jax.ShapeDtypeStruct(frames.shape, BF16),
        piece,
        piece,
        piece,
        piece,
        jax.ShapeDtypeStruct(weights.shape, BF16),
    )
    pin = lambda array: pltpu.with_memory_space_constraint(array, pltpu.HBM)
    vmem = pl.BlockSpec(memory_space=pltpu.VMEM)
    hbm = pl.BlockSpec(memory_space=pltpu.HBM)
    results = pl.pallas_call(
        functools.partial(step_kernel, n, frames_out),
        out_shape=outs,
        in_specs=[hbm] * 9,
        out_specs=[vmem] * 6,
        scratch_shapes=[
            pltpu.VMEM(frames.shape, BF16),
            pltpu.VMEM(weights.shape, BF16),
            pltpu.VMEM((1, chans), F32),
            pltpu.VMEM((1, chans), F32),
            pltpu.VMEM(projection.shape, BF16),
            pltpu.VMEM(targets.shape, F32),
            pltpu.VMEM(master.shape, F32),
            pltpu.VMEM(master.shape, F32),
            pltpu.VMEM(master.shape, F32),
            pltpu.VMEM((pad, 2 * chans), BF16),
            pltpu.VMEM((chans, 2 * chans), BF16),
            pltpu.VMEM((pad, chans), F32),
            pltpu.VMEM((pad, chans), F32),
            pltpu.VMEM((pad, chans), BF16),
            pltpu.VMEM((pad, 2 * chans), F32),
            pltpu.VMEM((2, depth, 2, 2, 2) + block, F32),
            pltpu.VMEM((depth, 2, 2, 2) + block, BF16),
            pltpu.VMEM((depth, 2, 2, 2) + block, BF16),
            pltpu.VMEM((depth, 3, 2) + block, BF16),
            pltpu.VMEM((depth, 3, 2) + block, BF16),
            pltpu.VMEM((depth, 2) + block, BF16),
            pltpu.VMEM((depth, 2) + block, BF16),
            pltpu.VMEM((1, LANES), F32),
            pltpu.VMEM((n - 1, LANES), F32),
            pltpu.VMEM(master.shape, F32),
            dma((9,)),
            dma((depth,)), dma((depth,)),
            dma((3 * depth,)), dma((3 * depth,)),
            dma((depth,)), dma((depth,)), dma((n - 1,)), dma((n - 1,)),
            dma((depth,)), dma((depth,)), dma((3 * depth,)), dma((3 * depth,)),
            dma((4 * depth,)), dma((4 * depth,)),
        ],
        compiler_params=pltpu.CompilerParams(
            collective_id=0, has_side_effects=True, vmem_limit_bytes=40 * 1024 * 1024
        ),
        name="conv_step",
    )(
        *map(
            pin,
            (
                frames, weights, ln_gain[None], ln_bias[None], projection, targets, master,
                first_moment, second_moment,
            ),
        )
    )
    results = pl.pallas_call(
        hand_over,
        out_shape=outs,
        in_specs=[vmem] * 6,
        out_specs=[hbm] * 6,
        scratch_shapes=[dma((6,))],
        compiler_params=pltpu.CompilerParams(vmem_limit_bytes=2 * 1024 * 1024),
        name="hand_over",
    )(*results)
    return (jnp.transpose(results[0], (1, 0, 2)),) + tuple(results[1:])


def body(n, *args):
    inputs, weights, master = args[0], args[1], args[6]
    chans, width = inputs.shape[2], master.shape[1]
    fits = (
        n % 8 == 0 and n > 8 and weights.shape[0] == 2 and 8 % inputs.shape[0] == 0
        and chans % (2 * LANES) == 0 and width % (16 * chans) == 0
        and chans % (LANES * (n // 8)) == 0
    )
    return kernel_body(n, *args) if fits else plain_body(*args)


def solution(mesh):
    return jax.shard_map(
        functools.partial(body, mesh.shape["dp"]),
        mesh=mesh,
        in_specs=(
            P("dp", None, None),
            P(),
            P(),
            P(),
            P(),
            P("dp", None),
            P(None, "dp"),
            P(None, "dp"),
            P(None, "dp"),
        ),
        out_specs=(
            P("dp", None, None),
            P(None, "dp"),
            P(None, "dp"),
            P(None, "dp"),
            P(None, "dp"),
            P(),
        ),
        check_vma=False,
    )
```

```python
import functools

import jax
import jax.numpy as jnp
from jax import lax
from jax.experimental import pallas as pl
from jax.experimental.pallas import tpu as pltpu
from jax.sharding import PartitionSpec as P

MESH = pl.DeviceIdType.MESH
LANES = 128
F32 = jnp.float32
BF16 = jnp.bfloat16


def norm_act(pre, gain, bias):
    center = pre - jnp.mean(pre, axis=-1, keepdims=True)
    spread = jnp.mean(center * center, axis=-1, keepdims=True)
    normed = center * lax.rsqrt(spread + 1e-05)
    return jax.nn.gelu(normed * gain + bias, approximate=False)


def local_pass(inputs, weights, ln_gain, ln_bias, projection, targets):
    clips, frames_in, chans = inputs.shape
    taps = weights.shape[0]
    frames_out = (frames_in - taps) // taps + 1
    windows = inputs[:, : frames_out * taps].reshape(clips, frames_out, taps, chans)
    kernel = weights.reshape(taps, chans, chans)
    pre = jnp.einsum("bfki,koi->bfo", windows, kernel, preferred_element_type=jnp.float32)
    act, pull = jax.vjp(lambda value: norm_act(value, ln_gain, ln_bias), pre)
    pooled = jnp.mean(act, axis=1).astype(jnp.bfloat16)
    predicted = jnp.dot(pooled, projection, preferred_element_type=jnp.float32)
    miss = (predicted - targets).astype(jnp.bfloat16)
    back = lax.dot_general(
        miss, projection, (((1,), (1,)), ((), ())), preferred_element_type=jnp.float32
    )
    upstream = jnp.broadcast_to(back[:, None, :] / frames_out, act.shape)
    dpre = pull(upstream)[0].astype(jnp.bfloat16)
    dwin = jnp.einsum("bfo,koi->bfki", dpre, kernel, preferred_element_type=jnp.float32).astype(
        jnp.bfloat16
    )
    dinput = dwin.reshape(clips, frames_out * taps, chans)
    tail = jnp.zeros((clips, frames_in - frames_out * taps, chans), jnp.bfloat16)
    return (windows, dpre, jnp.concatenate([dinput, tail], axis=1))


def adamw(grad, scale, master, first_moment, second_moment):
    clipped = scale * grad
    new_first = 0.9 * first_moment + 0.1 * clipped
    new_second = 0.999 * second_moment + 0.001 * clipped * clipped
    update = new_first / (1.0 - 0.9**20) / (jnp.sqrt(new_second / (1.0 - 0.999**20)) + 1e-08)
    new_master = master - 0.0001 * (update + 0.01 * master)
    return update, new_master, new_first, new_second


def plain_body(
    inputs, weights, ln_gain, ln_bias, projection, targets, master, first_moment, second_moment
):
    windows, dpre, input_grad = local_pass(inputs, weights, ln_gain, ln_bias, projection, targets)
    taps = weights.shape[0]
    term = jnp.einsum("bfo,bfki->koi", dpre, windows, preferred_element_type=jnp.float32)
    grad = lax.psum_scatter(term.reshape(taps, -1), "dp", scatter_dimension=1, tiled=True)
    squares = lax.psum(jnp.sum(grad * grad), "dp")
    scale = jnp.minimum(1.0, 1.0 / (jnp.sqrt(squares) + 1e-06))
    update, new_master, new_first, new_second = adamw(
        grad, scale, master, first_moment, second_moment
    )
    new_weights = lax.all_gather(new_master.astype(jnp.bfloat16), "dp", axis=1, tiled=True)
    return (input_grad, update, new_master, new_first, new_second, new_weights)


def dot(a, b, dims):
    return lax.dot_general(a, b, (dims, ((), ())), preferred_element_type=F32)


def step_kernel(
    n, frames_out,
    inputs_hbm, weights_hbm, gain_hbm, bias_hbm, projection_hbm, targets_hbm, master_hbm,
    first_hbm, second_hbm,
    dinput, update, new_master, new_first, new_second, gathered,
    inputs, weights, gain_ref, bias_ref, projection, targets, master, first, second,
    win, kern, pre_ref, slope, dpre_ref, dwin, term,
    out0, in0, out1, in1, out3, in3, sq_out, sq_in, grad,
    load, s0, r0, s1, r1, s3, r3, sq_s, sq_r, zs_s, zs_r, near_s, near_r, cs, cr,
):
    frames_in, clips, chans = inputs.shape
    live_rows = frames_out * clips
    pad_rows = win.shape[0]
    width = grad.shape[1]
    rows = width // chans
    depth = n // 8

    me = lax.axis_index("dp")
    c = me % 2
    x = (me // 2) % 2
    y = (me // 4) % 2
    z = me // 8
    core_peer = me + 1 - 2 * c
    x_peer = me + 2 - 4 * x
    y_peer = me + 4 - 8 * y
    near = (
        (1 - x, 1 - y, x_peer + y_peer - me),
        (1 - x, y, x_peer),
        (x, 1 - y, y_peer),
    )

    loads = [
        pltpu.make_async_copy(src, dst, load.at[k])
        for k, (src, dst) in enumerate(
            (
                (inputs_hbm, inputs), (weights_hbm, weights), (gain_hbm, gain_ref),
                (bias_hbm, bias_ref), (projection_hbm, projection), (targets_hbm, targets),
                (master_hbm, master), (first_hbm, first), (second_hbm, second),
            )
        )
    ]
    for copy in loads[:4]:
        copy.start()

    barrier = pltpu.get_barrier_semaphore()
    for j in range(1, n):
        pl.semaphore_signal(barrier, inc=1, device_id=((me + j) % n,), device_id_type=MESH)

    loads[0].wait()
    pairs = inputs[0 : 2 * frames_out].reshape(frames_out, 2, clips, chans)
    for t in range(2):
        win[0:live_rows, t * chans : (t + 1) * chans] = (
            pairs[:, t].reshape(live_rows, chans)
        )
    if pad_rows > live_rows:
        win[live_rows:pad_rows, :] = jnp.zeros((pad_rows - live_rows, 2 * chans), BF16)
    loads[1].wait()
    for copy in loads[4:]:
        copy.start()
    group = 64 if chans % 64 == 0 else 16

    @pl.loop(0, chans // group)
    def _(q):
        lanes = pl.ds(pl.multiple_of(q * group * chans, LANES), group * chans)
        flat = weights[:, lanes].reshape(2, group, chans)
        out = pl.ds(pl.multiple_of(q * group, group), group)
        for t in range(2):
            kern[out, t * chans : (t + 1) * chans] = flat[t]

    pre_ref[...] = dot(win[...], kern[...], ((1,), (1,)))
    loads[2].wait()
    loads[3].wait()
    gain = gain_ref[...]
    bias = bias_ref[...]
    step = 80 if pad_rows % 80 == 0 else 16

    def forward(i, fold):
        base = pl.multiple_of(i * step, 16)
        part = pl.ds(base, step)
        pre = pre_ref[part, :]
        center = pre - jnp.mean(pre, axis=-1, keepdims=True)
        spread = jnp.mean(center * center, axis=-1, keepdims=True)
        inv = lax.rsqrt(spread + 1e-05)
        nrm = center * inv
        h = nrm * gain + bias
        cdf = 0.5 + 0.5 * lax.erf(h * (0.5**0.5))
        pdf = jnp.exp(-0.5 * h * h) * 0.3989422804014327
        live = lax.broadcasted_iota(jnp.int32, (step, 1), 0) < live_rows - base
        act = jnp.where(live, h * cdf, 0.0)
        slope[part, :] = (cdf + h * pdf) * (gain * jnp.where(live, inv, 0.0))
        pre_ref[part, :] = nrm
        return fold + jnp.sum(act.reshape(step // 8, 8, chans), axis=0)

    fold = lax.fori_loop(0, pad_rows // step, forward, jnp.zeros((8, chans), F32))
    pooled = fold
    for k in range(1, 8 // clips):
        pooled = pooled + pltpu.roll(fold, k * clips, 0)
    pooled = (pooled / frames_out).astype(BF16)
    loads[4].wait()
    loads[5].wait()
    predicted = dot(pooled, projection[...], ((1,), (0,)))
    goal = jnp.concatenate([targets[...]] * (8 // clips), axis=0)
    miss = (predicted - goal).astype(BF16)
    back = dot(miss, projection[...], ((1,), (1,))) / frames_out

    @pl.loop(0, pad_rows // step)
    def _(i):
        part = pl.ds(pl.multiple_of(i * step, 16), step)
        nrm = pre_ref[part, :]
        dn = (slope[part, :].reshape(step // 8, 8, chans) * back[None]).reshape(step, chans)
        low = jnp.mean(dn, axis=-1, keepdims=True)
        tilt = jnp.mean(dn * nrm, axis=-1, keepdims=True)
        dpre_ref[part, :] = (dn - low - nrm * tilt).astype(BF16)

    def drain(ref, sem):
        pltpu.make_async_copy(ref, ref, sem).wait()

    def every(count):
        return gathered.at[:, pl.ds(0, count * width)]

    def send(src, dst, ssem, rsem, peer):
        copy = pltpu.make_async_remote_copy(
            src_ref=src, dst_ref=dst, send_sem=ssem, recv_sem=rsem,
            device_id=(peer,), device_id_type=MESH,
        )
        copy.start()
        return copy

    order = [(z + j) % depth for j in range(1, depth)] + [z]
    copies0 = []

    def to_core(k):
        zz = order[k]
        span = chans // depth
        value = dot(
            dpre_ref[:, pl.ds(pl.multiple_of(zz * span, LANES), span)], win[...], ((0,), (0,))
        )
        for d in range(8):
            for t in range(2):
                term[d % 2, zz, (d // 2) % 2, d // 4, t] = value[
                    d * rows : (d + 1) * rows, t * chans : (t + 1) * chans
                ]
        out0[zz] = term[1 - c, zz].astype(BF16)
        if k == 0:
            pl.semaphore_wait(barrier, n - 1)
        copies0.append(send(out0.at[zz], in0.at[zz], s0.at[k], r0.at[k], core_peer))

    def to_near(k):
        zz = order[k]
        copies0[k].wait_recv()
        for i, (xx, yy, peer) in enumerate(near):
            out1[zz, i] = (term[c, zz, xx, yy] + in0[zz, xx, yy].astype(F32)).astype(BF16)
            send(out1.at[zz, i], in1.at[zz, i], s1.at[k], r1.at[k], peer)

    for k in range(depth):
        to_core(k)
        if k:
            to_near(k - 1)
    to_near(depth - 1)
    dwin[...] = dot(dpre_ref[...], kern[...], ((1,), (0,)))

    def held(k):
        zz = order[k]
        drain(in1.at[zz], r1.at[k])
        value = term[c, zz, x, y] + in0[zz, x, y].astype(F32)
        for i in range(3):
            value = value + in1[zz, i].astype(F32)
        return value

    copies3 = []
    for k in range(depth - 1):
        out3[k] = held(k).astype(BF16)
        copies3.append(
            send(out3.at[k], in3.at[k], s3.at[k], r3.at[k], (me + 8 * (k + 1)) % n)
        )
    own = held(depth - 1)
    for k in range(depth - 1):
        copies3[k].wait_recv()
        own = own + in3[k].astype(F32)

    squares = own[0] * own[0] + own[1] * own[1]
    fold = sum(squares[:, l * LANES : (l + 1) * LANES] for l in range(chans // LANES))
    sq_out[...] = jnp.sum(fold, axis=0, keepdims=True)
    for j in range(1, n):
        send(sq_out, sq_in.at[pl.ds(j - 1, 1)], sq_s, sq_r, (me + j) % n)
    for r in range(rows):
        for t in range(2):
            grad[t : t + 1, r * chans : (r + 1) * chans] = own[t][r : r + 1, :]
    for k in range(6, 9):
        loads[k].wait()
    taps = [
        dwin[0:live_rows, t * chans : (t + 1) * chans]
        .astype(BF16)
        .reshape(frames_out, 1, clips, chans)
        for t in range(2)
    ]
    dinput[0 : 2 * frames_out] = jnp.concatenate(taps, axis=1).reshape(
        2 * frames_out, clips, chans
    )
    if frames_in > 2 * frames_out:
        dinput[2 * frames_out : frames_in] = jnp.zeros(
            (frames_in - 2 * frames_out, clips, chans), BF16
        )
    for k, zz in enumerate(order):
        drain(out1.at[zz], s1.at[k])
    for copy in copies0 + copies3:
        copy.wait_send()
    drain(sq_in, sq_r)
    total = jnp.sum(sq_in[...]) + jnp.sum(sq_out[...])
    scale = jnp.minimum(1.0, 1.0 / (jnp.sqrt(jnp.full((1, 1), total)) + 1e-06))

    upd, nm, nf, ns = adamw(grad[...], scale, master[...], first[...], second[...])

    def piece(zz, yy, xx):
        start = (((zz * 2 + yy) * 2 + xx) * 2 + c) * width
        return gathered.at[:, pl.ds(pl.multiple_of(start, LANES), width)]

    mine = piece(z, y, x)
    mine[...] = nm.astype(BF16)

    arrive = []
    for j in range(1, depth):
        copy = send(mine, mine, zs_s.at[j - 1], zs_r.at[j - 1], (me + 8 * j) % n)
        arrive.append(copy)
    around = []
    for j in range(depth):
        zz = (z + depth - j) % depth
        if j:
            arrive[j - 1].wait_recv()
        block = piece(zz, y, x)
        around.append(
            [
                send(block, block, near_s, near_r.at[3 * j + i], peer)
                for i, (xx, yy, peer) in enumerate(near)
            ]
        )
        send(block, block, cs, cr, core_peer)
        if j == 0:
            update[...] = upd
            new_master[...] = nm
            new_first[...] = nf
            new_second[...] = ns
            drain(sq_in, sq_s)
    for j in range(depth):
        zz = (z + depth - j) % depth
        for i in (1, 2, 0):
            around[j][i].wait_recv()
            block = piece(zz, near[i][1], near[i][0])
            send(block, block, cs, cr, core_peer)
    for copy in arrive:
        copy.wait_send()
    drain(every(3 * depth), near_s)
    drain(every(4 * depth), cs)
    drain(every(4 * depth), cr)


def hand_over(*refs):
    count = (len(refs) - 1) // 2
    sems = refs[-1]
    copies = [
        pltpu.make_async_copy(refs[k], refs[count + k], sems.at[k]) for k in range(count)
    ]
    for copy in copies:
        copy.start()
    for copy in copies:
        copy.wait()


def kernel_body(
    n, inputs, weights, ln_gain, ln_bias, projection, targets, master, first_moment, second_moment
):
    clips, frames_in, chans = inputs.shape
    taps = weights.shape[0]
    frames_out = (frames_in - taps) // taps + 1
    width = master.shape[1]
    rows = width // chans
    depth = n // 8
    pad = -(-clips * frames_out // 16) * 16
    dma = pltpu.SemaphoreType.DMA
    block = (rows, chans)
    piece = jax.ShapeDtypeStruct(master.shape, F32)
    frames = jnp.transpose(inputs, (1, 0, 2))
    outs = (
        jax.ShapeDtypeStruct(frames.shape, BF16),
        piece,
        piece,
        piece,
        piece,
        jax.ShapeDtypeStruct(weights.shape, BF16),
    )
    pin = lambda array: pltpu.with_memory_space_constraint(array, pltpu.HBM)
    vmem = pl.BlockSpec(memory_space=pltpu.VMEM)
    hbm = pl.BlockSpec(memory_space=pltpu.HBM)
    results = pl.pallas_call(
        functools.partial(step_kernel, n, frames_out),
        out_shape=outs,
        in_specs=[hbm] * 9,
        out_specs=[vmem] * 6,
        scratch_shapes=[
            pltpu.VMEM(frames.shape, BF16),
            pltpu.VMEM(weights.shape, BF16),
            pltpu.VMEM((1, chans), F32),
            pltpu.VMEM((1, chans), F32),
            pltpu.VMEM(projection.shape, BF16),
            pltpu.VMEM(targets.shape, F32),
            pltpu.VMEM(master.shape, F32),
            pltpu.VMEM(master.shape, F32),
            pltpu.VMEM(master.shape, F32),
            pltpu.VMEM((pad, 2 * chans), BF16),
            pltpu.VMEM((chans, 2 * chans), BF16),
            pltpu.VMEM((pad, chans), F32),
            pltpu.VMEM((pad, chans), F32),
            pltpu.VMEM((pad, chans), BF16),
            pltpu.VMEM((pad, 2 * chans), F32),
            pltpu.VMEM((2, depth, 2, 2, 2) + block, F32),
            pltpu.VMEM((depth, 2, 2, 2) + block, BF16),
            pltpu.VMEM((depth, 2, 2, 2) + block, BF16),
            pltpu.VMEM((depth, 3, 2) + block, BF16),
            pltpu.VMEM((depth, 3, 2) + block, BF16),
            pltpu.VMEM((depth, 2) + block, BF16),
            pltpu.VMEM((depth, 2) + block, BF16),
            pltpu.VMEM((1, LANES), F32),
            pltpu.VMEM((n - 1, LANES), F32),
            pltpu.VMEM(master.shape, F32),
            dma((9,)),
            dma((depth,)), dma((depth,)),
            dma((depth,)), dma((depth,)),
            dma((depth,)), dma((depth,)), dma, dma,
            dma((depth,)), dma((depth,)), dma, dma((3 * depth,)),
            dma, dma,
        ],
        compiler_params=pltpu.CompilerParams(
            collective_id=0, has_side_effects=True, vmem_limit_bytes=40 * 1024 * 1024
        ),
        name="conv_step",
    )(
        *map(
            pin,
            (
                frames, weights, ln_gain[None], ln_bias[None], projection, targets, master,
                first_moment, second_moment,
            ),
        )
    )
    results = pl.pallas_call(
        hand_over,
        out_shape=outs,
        in_specs=[vmem] * 6,
        out_specs=[hbm] * 6,
        scratch_shapes=[dma((6,))],
        compiler_params=pltpu.CompilerParams(vmem_limit_bytes=2 * 1024 * 1024),
        name="hand_over",
    )(*results)
    return (jnp.transpose(results[0], (1, 0, 2)),) + tuple(results[1:])


def body(n, *args):
    inputs, weights, master = args[0], args[1], args[6]
    chans, width = inputs.shape[2], master.shape[1]
    fits = (
        n % 8 == 0 and n > 8 and weights.shape[0] == 2 and 8 % inputs.shape[0] == 0
        and chans % (2 * LANES) == 0 and width % (16 * chans) == 0
        and chans % (LANES * (n // 8)) == 0
    )
    return kernel_body(n, *args) if fits else plain_body(*args)


def solution(mesh):
    return jax.shard_map(
        functools.partial(body, mesh.shape["dp"]),
        mesh=mesh,
        in_specs=(
            P("dp", None, None),
            P(),
            P(),
            P(),
            P(),
            P("dp", None),
            P(None, "dp"),
            P(None, "dp"),
            P(None, "dp"),
        ),
        out_specs=(
            P("dp", None, None),
            P(None, "dp"),
            P(None, "dp"),
            P(None, "dp"),
            P(None, "dp"),
            P(),
        ),
        check_vma=False,
    )
```

```python
import functools

import jax
import jax.numpy as jnp
from jax import lax
from jax.experimental import pallas as pl
from jax.experimental.pallas import tpu as pltpu
from jax.sharding import PartitionSpec as P

MESH = pl.DeviceIdType.MESH
LANES = 128
F32 = jnp.float32
BF16 = jnp.bfloat16


def norm_act(pre, gain, bias):
    center = pre - jnp.mean(pre, axis=-1, keepdims=True)
    spread = jnp.mean(center * center, axis=-1, keepdims=True)
    normed = center * lax.rsqrt(spread + 1e-05)
    return jax.nn.gelu(normed * gain + bias, approximate=False)


def local_pass(inputs, weights, ln_gain, ln_bias, projection, targets):
    clips, frames_in, chans = inputs.shape
    taps = weights.shape[0]
    frames_out = (frames_in - taps) // taps + 1
    windows = inputs[:, : frames_out * taps].reshape(clips, frames_out, taps, chans)
    kernel = weights.reshape(taps, chans, chans)
    pre = jnp.einsum("bfki,koi->bfo", windows, kernel, preferred_element_type=jnp.float32)
    act, pull = jax.vjp(lambda value: norm_act(value, ln_gain, ln_bias), pre)
    pooled = jnp.mean(act, axis=1).astype(jnp.bfloat16)
    predicted = jnp.dot(pooled, projection, preferred_element_type=jnp.float32)
    miss = (predicted - targets).astype(jnp.bfloat16)
    back = lax.dot_general(
        miss, projection, (((1,), (1,)), ((), ())), preferred_element_type=jnp.float32
    )
    upstream = jnp.broadcast_to(back[:, None, :] / frames_out, act.shape)
    dpre = pull(upstream)[0].astype(jnp.bfloat16)
    dwin = jnp.einsum("bfo,koi->bfki", dpre, kernel, preferred_element_type=jnp.float32).astype(
        jnp.bfloat16
    )
    dinput = dwin.reshape(clips, frames_out * taps, chans)
    tail = jnp.zeros((clips, frames_in - frames_out * taps, chans), jnp.bfloat16)
    return (windows, dpre, jnp.concatenate([dinput, tail], axis=1))


def adamw(grad, scale, master, first_moment, second_moment):
    clipped = scale * grad
    new_first = 0.9 * first_moment + 0.1 * clipped
    new_second = 0.999 * second_moment + 0.001 * clipped * clipped
    update = new_first / (1.0 - 0.9**20) / (jnp.sqrt(new_second / (1.0 - 0.999**20)) + 1e-08)
    new_master = master - 0.0001 * (update + 0.01 * master)
    return update, new_master, new_first, new_second


def plain_body(
    inputs, weights, ln_gain, ln_bias, projection, targets, master, first_moment, second_moment
):
    windows, dpre, input_grad = local_pass(inputs, weights, ln_gain, ln_bias, projection, targets)
    taps = weights.shape[0]
    term = jnp.einsum("bfo,bfki->koi", dpre, windows, preferred_element_type=jnp.float32)
    grad = lax.psum_scatter(term.reshape(taps, -1), "dp", scatter_dimension=1, tiled=True)
    squares = lax.psum(jnp.sum(grad * grad), "dp")
    scale = jnp.minimum(1.0, 1.0 / (jnp.sqrt(squares) + 1e-06))
    update, new_master, new_first, new_second = adamw(
        grad, scale, master, first_moment, second_moment
    )
    new_weights = lax.all_gather(new_master.astype(jnp.bfloat16), "dp", axis=1, tiled=True)
    return (input_grad, update, new_master, new_first, new_second, new_weights)


def dot(a, b, dims):
    return lax.dot_general(a, b, (dims, ((), ())), preferred_element_type=F32)


def step_kernel(
    n, frames_out,
    inputs_hbm, weights_hbm, gain_hbm, bias_hbm, projection_hbm, targets_hbm, master_hbm,
    first_hbm, second_hbm,
    dinput, update, new_master, new_first, new_second, gathered,
    inputs, weights, gain_ref, bias_ref, projection, targets, master, first, second,
    win, kern, pre_ref, slope, dpre_ref, dwin, term,
    out0, in0, out1, in1, out3, in3, sq_out, sq_in, grad,
    load, s0, r0, s1, r1, s3, r3, sq_s, sq_r, zs_s, zs_r, near_s, near_r, cs, cr,
):
    frames_in, clips, chans = inputs.shape
    live_rows = frames_out * clips
    pad_rows = win.shape[0]
    width = grad.shape[1]
    rows = width // chans
    depth = n // 8

    me = lax.axis_index("dp")
    c = me % 2
    x = (me // 2) % 2
    y = (me // 4) % 2
    z = me // 8
    core_peer = me + 1 - 2 * c
    x_peer = me + 2 - 4 * x
    y_peer = me + 4 - 8 * y
    near = (
        (1 - x, 1 - y, x_peer + y_peer - me),
        (1 - x, y, x_peer),
        (x, 1 - y, y_peer),
    )

    loads = [
        pltpu.make_async_copy(src, dst, load.at[k])
        for k, (src, dst) in enumerate(
            (
                (inputs_hbm, inputs), (weights_hbm, weights), (gain_hbm, gain_ref),
                (bias_hbm, bias_ref), (projection_hbm, projection), (targets_hbm, targets),
                (master_hbm, master), (first_hbm, first), (second_hbm, second),
            )
        )
    ]
    for copy in loads[:4]:
        copy.start()

    barrier = pltpu.get_barrier_semaphore()
    for j in range(1, n):
        pl.semaphore_signal(barrier, inc=1, device_id=((me + j) % n,), device_id_type=MESH)

    loads[0].wait()
    pairs = inputs[0 : 2 * frames_out].reshape(frames_out, 2, clips, chans)
    for t in range(2):
        win[0:live_rows, t * chans : (t + 1) * chans] = (
            pairs[:, t].reshape(live_rows, chans)
        )
    if pad_rows > live_rows:
        win[live_rows:pad_rows, :] = jnp.zeros((pad_rows - live_rows, 2 * chans), BF16)
    loads[1].wait()
    for copy in loads[4:]:
        copy.start()
    group = 64 if chans % 64 == 0 else 16

    @pl.loop(0, chans // group)
    def _(q):
        lanes = pl.ds(pl.multiple_of(q * group * chans, LANES), group * chans)
        flat = weights[:, lanes].reshape(2, group, chans)
        out = pl.ds(pl.multiple_of(q * group, group), group)
        for t in range(2):
            kern[out, t * chans : (t + 1) * chans] = flat[t]

    pre_ref[...] = dot(win[...], kern[...], ((1,), (1,)))
    loads[2].wait()
    loads[3].wait()
    gain = gain_ref[...]
    bias = bias_ref[...]
    step = 80 if pad_rows % 80 == 0 else 16

    short = step // 2

    def forward(i, fold):
        base = pl.multiple_of(i * short, 8)
        part = pl.ds(base, short)
        pre = pre_ref[part, :]
        center = pre - jnp.mean(pre, axis=-1, keepdims=True)
        spread = jnp.mean(center * center, axis=-1, keepdims=True)
        inv = lax.rsqrt(spread + 1e-05)
        nrm = center * inv
        h = nrm * gain + bias
        cdf = 0.5 + 0.5 * lax.erf(h * (0.5**0.5))
        pdf = jnp.exp(-0.5 * h * h) * 0.3989422804014327
        live = lax.broadcasted_iota(jnp.int32, (short, 1), 0) < live_rows - base
        act = jnp.where(live, h * cdf, 0.0)
        slope[part, :] = (cdf + h * pdf) * (gain * jnp.where(live, inv, 0.0))
        pre_ref[part, :] = nrm
        return fold + jnp.sum(act.reshape(short // 8, 8, chans), axis=0)

    fold = lax.fori_loop(0, pad_rows // short, forward, jnp.zeros((8, chans), F32))
    pooled = fold
    for k in range(1, 8 // clips):
        pooled = pooled + pltpu.roll(fold, k * clips, 0)
    pooled = (pooled / frames_out).astype(BF16)
    loads[4].wait()
    loads[5].wait()
    predicted = dot(pooled, projection[...], ((1,), (0,)))
    goal = jnp.concatenate([targets[...]] * (8 // clips), axis=0)
    miss = (predicted - goal).astype(BF16)
    back = dot(miss, projection[...], ((1,), (1,))) / frames_out

    @pl.loop(0, pad_rows // step)
    def _(i):
        part = pl.ds(pl.multiple_of(i * step, 16), step)
        nrm = pre_ref[part, :]
        dn = (slope[part, :].reshape(step // 8, 8, chans) * back[None]).reshape(step, chans)
        low = jnp.mean(dn, axis=-1, keepdims=True)
        tilt = jnp.mean(dn * nrm, axis=-1, keepdims=True)
        dpre_ref[part, :] = (dn - low - nrm * tilt).astype(BF16)

    def drain(ref, sem):
        pltpu.make_async_copy(ref, ref, sem).wait()

    def every(count):
        return gathered.at[:, pl.ds(0, count * width)]

    def send(src, dst, ssem, rsem, peer):
        copy = pltpu.make_async_remote_copy(
            src_ref=src, dst_ref=dst, send_sem=ssem, recv_sem=rsem,
            device_id=(peer,), device_id_type=MESH,
        )
        copy.start()
        return copy

    order = [(z + j) % depth for j in range(1, depth)] + [z]
    copies0 = []

    def to_core(k):
        zz = order[k]
        span = chans // depth
        value = dot(
            dpre_ref[:, pl.ds(pl.multiple_of(zz * span, LANES), span)], win[...], ((0,), (0,))
        )
        for d in range(8):
            for t in range(2):
                term[d % 2, zz, (d // 2) % 2, d // 4, t] = value[
                    d * rows : (d + 1) * rows, t * chans : (t + 1) * chans
                ]
        out0[zz] = term[1 - c, zz].astype(BF16)
        if k == 0:
            pl.semaphore_wait(barrier, n - 1)
        copies0.append(send(out0.at[zz], in0.at[zz], s0.at[k], r0.at[k], core_peer))

    def to_near(k):
        zz = order[k]
        copies0[k].wait_recv()
        for i, (xx, yy, peer) in enumerate(near):
            out1[zz, i] = (term[c, zz, xx, yy] + in0[zz, xx, yy].astype(F32)).astype(BF16)
            send(out1.at[zz, i], in1.at[zz, i], s1.at[k], r1.at[k], peer)

    for k in range(depth):
        to_core(k)
        if k:
            to_near(k - 1)
    to_near(depth - 1)
    dwin[...] = dot(dpre_ref[...], kern[...], ((1,), (0,)))

    def held(k):
        zz = order[k]
        drain(in1.at[zz], r1.at[k])
        value = term[c, zz, x, y] + in0[zz, x, y].astype(F32)
        for i in range(3):
            value = value + in1[zz, i].astype(F32)
        return value

    copies3 = []
    for k in range(depth - 1):
        out3[k] = held(k).astype(BF16)
        copies3.append(
            send(out3.at[k], in3.at[k], s3.at[k], r3.at[k], (me + 8 * (k + 1)) % n)
        )
    own = held(depth - 1)
    for k in range(depth - 1):
        copies3[k].wait_recv()
        own = own + in3[k].astype(F32)

    squares = own[0] * own[0] + own[1] * own[1]
    fold = sum(squares[:, l * LANES : (l + 1) * LANES] for l in range(chans // LANES))
    sq_out[...] = jnp.sum(fold, axis=0, keepdims=True)
    for j in range(1, n):
        send(sq_out, sq_in.at[pl.ds(j - 1, 1)], sq_s, sq_r, (me + j) % n)
    for r in range(rows):
        for t in range(2):
            grad[t : t + 1, r * chans : (r + 1) * chans] = own[t][r : r + 1, :]
    for k in range(6, 9):
        loads[k].wait()
    taps = [
        dwin[0:live_rows, t * chans : (t + 1) * chans]
        .astype(BF16)
        .reshape(frames_out, 1, clips, chans)
        for t in range(2)
    ]
    dinput[0 : 2 * frames_out] = jnp.concatenate(taps, axis=1).reshape(
        2 * frames_out, clips, chans
    )
    if frames_in > 2 * frames_out:
        dinput[2 * frames_out : frames_in] = jnp.zeros(
            (frames_in - 2 * frames_out, clips, chans), BF16
        )
    for k, zz in enumerate(order):
        drain(out1.at[zz], s1.at[k])
    for copy in copies0 + copies3:
        copy.wait_send()
    drain(sq_in, sq_r)
    total = jnp.sum(sq_in[...]) + jnp.sum(sq_out[...])
    scale = jnp.minimum(1.0, 1.0 / (jnp.sqrt(jnp.full((1, 1), total)) + 1e-06))

    upd, nm, nf, ns = adamw(grad[...], scale, master[...], first[...], second[...])

    def piece(zz, yy, xx):
        start = (((zz * 2 + yy) * 2 + xx) * 2 + c) * width
        return gathered.at[:, pl.ds(pl.multiple_of(start, LANES), width)]

    mine = piece(z, y, x)
    mine[...] = nm.astype(BF16)

    arrive = []
    for j in range(1, depth):
        copy = send(mine, mine, zs_s.at[j - 1], zs_r.at[j - 1], (me + 8 * j) % n)
        arrive.append(copy)
    around = []
    for j in range(depth):
        zz = (z + depth - j) % depth
        if j:
            arrive[j - 1].wait_recv()
        block = piece(zz, y, x)
        around.append(
            [
                send(block, block, near_s, near_r.at[3 * j + i], peer)
                for i, (xx, yy, peer) in enumerate(near)
            ]
        )
        send(block, block, cs, cr, core_peer)
        if j == 0:
            update[...] = upd
            new_master[...] = nm
            new_first[...] = nf
            new_second[...] = ns
            drain(sq_in, sq_s)
    for j in range(depth):
        zz = (z + depth - j) % depth
        for i in (1, 2, 0):
            around[j][i].wait_recv()
            block = piece(zz, near[i][1], near[i][0])
            send(block, block, cs, cr, core_peer)
    for copy in arrive:
        copy.wait_send()
    drain(every(3 * depth), near_s)
    drain(every(4 * depth), cs)
    drain(every(4 * depth), cr)


def hand_over(*refs):
    count = (len(refs) - 1) // 2
    sems = refs[-1]
    copies = [
        pltpu.make_async_copy(refs[k], refs[count + k], sems.at[k]) for k in range(count)
    ]
    for copy in copies:
        copy.start()
    for copy in copies:
        copy.wait()


def kernel_body(
    n, inputs, weights, ln_gain, ln_bias, projection, targets, master, first_moment, second_moment
):
    clips, frames_in, chans = inputs.shape
    taps = weights.shape[0]
    frames_out = (frames_in - taps) // taps + 1
    width = master.shape[1]
    rows = width // chans
    depth = n // 8
    pad = -(-clips * frames_out // 16) * 16
    dma = pltpu.SemaphoreType.DMA
    block = (rows, chans)
    piece = jax.ShapeDtypeStruct(master.shape, F32)
    frames = jnp.transpose(inputs, (1, 0, 2))
    outs = (
        jax.ShapeDtypeStruct(frames.shape, BF16),
        piece,
        piece,
        piece,
        piece,
        jax.ShapeDtypeStruct(weights.shape, BF16),
    )
    pin = lambda array: pltpu.with_memory_space_constraint(array, pltpu.HBM)
    vmem = pl.BlockSpec(memory_space=pltpu.VMEM)
    hbm = pl.BlockSpec(memory_space=pltpu.HBM)
    results = pl.pallas_call(
        functools.partial(step_kernel, n, frames_out),
        out_shape=outs,
        in_specs=[hbm] * 9,
        out_specs=[vmem] * 6,
        scratch_shapes=[
            pltpu.VMEM(frames.shape, BF16),
            pltpu.VMEM(weights.shape, BF16),
            pltpu.VMEM((1, chans), F32),
            pltpu.VMEM((1, chans), F32),
            pltpu.VMEM(projection.shape, BF16),
            pltpu.VMEM(targets.shape, F32),
            pltpu.VMEM(master.shape, F32),
            pltpu.VMEM(master.shape, F32),
            pltpu.VMEM(master.shape, F32),
            pltpu.VMEM((pad, 2 * chans), BF16),
            pltpu.VMEM((chans, 2 * chans), BF16),
            pltpu.VMEM((pad, chans), F32),
            pltpu.VMEM((pad, chans), F32),
            pltpu.VMEM((pad, chans), BF16),
            pltpu.VMEM((pad, 2 * chans), F32),
            pltpu.VMEM((2, depth, 2, 2, 2) + block, F32),
            pltpu.VMEM((depth, 2, 2, 2) + block, BF16),
            pltpu.VMEM((depth, 2, 2, 2) + block, BF16),
            pltpu.VMEM((depth, 3, 2) + block, BF16),
            pltpu.VMEM((depth, 3, 2) + block, BF16),
            pltpu.VMEM((depth, 2) + block, BF16),
            pltpu.VMEM((depth, 2) + block, BF16),
            pltpu.VMEM((1, LANES), F32),
            pltpu.VMEM((n - 1, LANES), F32),
            pltpu.VMEM(master.shape, F32),
            dma((9,)),
            dma((depth,)), dma((depth,)),
            dma((depth,)), dma((depth,)),
            dma((depth,)), dma((depth,)), dma, dma,
            dma((depth,)), dma((depth,)), dma, dma((3 * depth,)),
            dma, dma,
        ],
        compiler_params=pltpu.CompilerParams(
            collective_id=0, has_side_effects=True, vmem_limit_bytes=40 * 1024 * 1024
        ),
        name="conv_step",
    )(
        *map(
            pin,
            (
                frames, weights, ln_gain[None], ln_bias[None], projection, targets, master,
                first_moment, second_moment,
            ),
        )
    )
    results = pl.pallas_call(
        hand_over,
        out_shape=outs,
        in_specs=[vmem] * 6,
        out_specs=[hbm] * 6,
        scratch_shapes=[dma((6,))],
        compiler_params=pltpu.CompilerParams(vmem_limit_bytes=2 * 1024 * 1024),
        name="hand_over",
    )(*results)
    return (jnp.transpose(results[0], (1, 0, 2)),) + tuple(results[1:])


def body(n, *args):
    inputs, weights, master = args[0], args[1], args[6]
    chans, width = inputs.shape[2], master.shape[1]
    fits = (
        n % 8 == 0 and n > 8 and weights.shape[0] == 2 and 8 % inputs.shape[0] == 0
        and chans % (2 * LANES) == 0 and width % (16 * chans) == 0
        and chans % (LANES * (n // 8)) == 0
    )
    return kernel_body(n, *args) if fits else plain_body(*args)


def solution(mesh):
    return jax.shard_map(
        functools.partial(body, mesh.shape["dp"]),
        mesh=mesh,
        in_specs=(
            P("dp", None, None),
            P(),
            P(),
            P(),
            P(),
            P("dp", None),
            P(None, "dp"),
            P(None, "dp"),
            P(None, "dp"),
        ),
        out_specs=(
            P("dp", None, None),
            P(None, "dp"),
            P(None, "dp"),
            P(None, "dp"),
            P(None, "dp"),
            P(),
        ),
        check_vma=False,
    )
```
